128 devices in a mesh: grp: 2 (over y_lo), dev: 64 (over y_hi, z, x, core).
Axes of the slice: x: 4, y: 4 (y_hi: 2, y_lo: 2; y = y_hi * 2 + y_lo), z: 4, core: 2. Of those that a mesh axis runs over, the one named last changes fastest.
Arguments:
- queries: bfloat16 [256, 128, 576], P(('grp', 'dev')), may hold values from -240 to 240
- cache: bfloat16 [256, 2048, 576], P(('grp', 'dev')), may hold values from -6 to 6
- lengths: int32 [256], P(('grp', 'dev')), may hold values from 1 to 2048, 131072 in all
- w_uv: bfloat16 [128, 512, 128], P(('grp', 'dev')), may hold values from -3 to 3
- w_out: bfloat16 [16384, 7168], P(('grp', 'dev')), may hold values from -0.046875 to 0.046875
- residual: bfloat16 [256, 7168], P(('grp', 'dev')), may hold values from -3 to 3
- gain: float32 [7168], replicated, may hold values from 0.5 to 1.5
- ids: int32 [256, 8], P(('grp', 'dev')), may hold values from 0 to 31, all different within a row; in each aligned block of 2 rows (0 to 1, 2 to 3, ...) at most 2 rows name the same one
- gates: float32 [256, 8], P(('grp', 'dev')), may hold values from 0.05 to 0.5
- w_gate: bfloat16 [128, 7168, 256], P(('grp', 'dev')), may hold values from -0.0625 to 0.0625
- w_up: bfloat16 [128, 7168, 256], P(('grp', 'dev')), may hold values from -0.0625 to 0.0625
- w_down: bfloat16 [128, 256, 7168], P(('grp', 'dev')), may hold values from -0.1875 to 0.1875
Outputs:
- layer_out: bfloat16 [256, 7168], P(('grp', 'dev'))
The draws below stay inside these ranges and needn't reach their ends.
Inputs may be any that keep to these rules, and one draw needn't show every extreme that they name: `ids`: among the rows of one device no expert is named by more than 2 rows, a bound that some block reaches. `lengths`: some request has all 2048 slots live.
All inputs are finite; a program needn't handle non-finite values. No bound on the sum of `lengths` on one device may be relied on, other than what follows from the above.
Results may differ from the reference program's by a relative error of at most 0.006.
Values may be sent and summed in bfloat16 or wider, within the bound.
No kernel may reach another device: no remote copies, remote signals or barrier semaphores. Data moves between devices by JAX's collectives and lax.ppermute only.
A program may use at most 128 MiB of HBM per device.

```python
import math
import jax
import jax.numpy as jnp
import numpy as np
from jax import lax

D = 7168
HEADS = 128
LATENT = 512
ROPE = 64
VHEAD = 128
TOP = 8
MOE_FF = 1024
HID_DEV = 256
R_DEV = 2
L_MAX = 2048
SLICES = 4
EXPERTS = 32
CAP = 2
REQUESTS = 256
DEVICES = 128


def draw_queries(key, part):
    key = jax.random.fold_in(key, 11)
    first = jax.random.fold_in(key, 0)
    base = jnp.clip(jax.random.normal(first, (REQUESTS, HEADS, LATENT + ROPE), jnp.float32), -4.0, 4.0)
    return base.astype(jnp.bfloat16)


def levels(rng, extent, cuts, least, top_value):
    factor_of, own = 1.0, jax.random.fold_in(rng, 6)
    for position, shards_of in cuts:
        draws = jnp.exp(jax.random.uniform(jax.random.fold_in(own, position), (shards_of,), jnp.float32, least / len(cuts), top_value / len(cuts)))
        factor_of = factor_of * jnp.repeat(draws, extent[position] // shards_of).reshape([-1 if axis == position else 1 for axis in range(len(extent))])
    return factor_of


def length_profile(number_of, total, reach, lean):
    portions = [(1 << 20) // math.isqrt(rank ** lean) + 1 for rank in range(2, number_of + 1)]
    rest, given = total - reach - (number_of - 1), [1] * (number_of - 1)
    while rest > 0:
        candidates = [i for i in range(number_of - 1) if given[i] < reach]
        whole, remaining = sum([portions[i] for i in candidates]), rest
        for i in candidates:
            addition = min(reach - given[i], max(1, remaining * portions[i] // whole), rest)
            given[i] = given[i] + addition
            rest = rest - addition
    return np.array([reach] + given)


def uneven_parts(stream_key, number_of, total, bound, slope):
    if number_of == 2:
        one = jax.random.randint(stream_key, (), max(1, total - bound), min(bound, total - 1) + 1)
        return jnp.stack([one, total - one])
    tallies = jnp.asarray(length_profile(number_of, total, bound, slope), jnp.int32)
    couples = (number_of - 1) // 2
    source_of, receiver = tallies[1:1 + 2 * couples:2], tallies[2:2 + 2 * couples:2]
    room = jnp.minimum(source_of - 1, bound - receiver)
    shifted = jax.random.randint(jax.random.fold_in(stream_key, 1), (couples,), 0, 1 << 20) % (room + 1)
    tallies = tallies.at[1:1 + 2 * couples:2].set(source_of - shifted).at[2:2 + 2 * couples:2].set(receiver + shifted)
    return tallies[jax.random.permutation(jax.random.fold_in(stream_key, 2), number_of)]


def shared_out(key, own, number, rows, count, top, bound, skew):
    order = jax.random.permutation(key, count)
    packed, common = shares(count, rows * top, bound, skew, True), shares(count, rows * top, bound, skew, False)
    places = jnp.arange(count)

    def named(sizes, offset_by):
        used = int((sizes > 0).sum())
        fixed = max(1, used // 4)
        passed = fixed + (places - fixed + offset_by * (used - fixed)) % max(1, count - fixed)
        return jnp.zeros((count,), jnp.int32).at[order[jnp.where(places < fixed, places, passed)]].set(jnp.asarray(sizes, jnp.int32))

    sizes = jnp.where(number % 4 == 0, named(packed, number // 4), named(common, number - number // 4 - 1))
    mixed = jax.random.permutation(jax.random.fold_in(own, 3), count)
    donor, receiver = mixed[0:count // 2 * 2:2], mixed[1:count // 2 * 2:2]
    slack = jnp.minimum(sizes[donor] - 1, bound - sizes[receiver]) // 2
    slack = jnp.where((donor == order[0]) | (receiver == order[0]) | (sizes[receiver] == 0), 0, jnp.maximum(slack, 0))
    passed = jax.random.randint(jax.random.fold_in(own, 4), (count // 2,), 0, 1 << 20) % (slack + 1)
    sizes = sizes.at[donor].add(-passed).at[receiver].add(passed)
    members = jnp.searchsorted(jnp.cumsum(sizes), jnp.arange(rows * top), side="right").astype(jnp.int32)
    table = members.reshape(top, rows).T
    table = table[jax.random.permutation(jax.random.fold_in(own, 1), rows)]
    offset_by = jax.random.randint(jax.random.fold_in(own, 2), (rows, 1), 0, top)
    return jnp.take_along_axis(table, (jnp.arange(top)[None, :] + offset_by) % top, axis=1)


def shares(count, total, bound, lean, full):
    weights = [(1 << 20) // math.isqrt(grade ** lean) + 1 for grade in range(1, count + 1)]
    largest = bound if full else min(bound, max(-(-total // count), total * weights[0] // sum(weights)))
    least = 1 if total - largest >= count - 1 else 0
    given, rest = [largest] + [least] * (count - 1), total - largest - least * (count - 1)
    while rest > 0:
        free = [i for i in range(1, count) if given[i] < largest] or [i for i in range(1, count) if given[i] < bound]
        pool, remaining = sum([weights[i] for i in free]), rest
        for i in free:
            more = min(bound - given[i], max(1, remaining * weights[i] // pool), rest)
            given[i] = given[i] + more
            rest = rest - more
    return np.array(given)


def gaussian(rng, extent, width, limit, cuts=(), held_as=jnp.bfloat16):
    entries = width * jax.random.normal(rng, extent, jnp.float32)
    if cuts:
        entries = entries * levels(rng, extent, cuts, -0.22, 0.18)
    return jnp.clip(entries, -limit, limit).astype(held_as)


def setup_inputs(seed: int = 0) -> dict:
    key_of = jax.random.split(jax.random.key(seed), 13)
    queries = draw_queries(jax.random.fold_in(key_of[12], 71), 0)
    cache = gaussian(key_of[1], (REQUESTS, L_MAX, LATENT + ROPE), 1.0, 6.0, ((0, 128),))
    lengths = uneven_parts(key_of[2], REQUESTS, REQUESTS * L_MAX // 4, L_MAX, 2).astype(jnp.int32)
    w_uv = gaussian(key_of[3], (HEADS, LATENT, VHEAD), 0.5, 3.0, ((0, 128),))
    w_out = gaussian(key_of[4], (HEADS * VHEAD, D), (HEADS * VHEAD) ** -0.5, 0.046875, ((0, 128),))
    residual = gaussian(key_of[5], (REQUESTS, D), 0.5, 3.0, ((0, 128),))
    gain = jnp.clip(1.0 + 0.1 * jax.random.normal(key_of[6], (D,), jnp.float32), 0.5, 1.5)
    ids_keys = jax.random.split(jax.random.fold_in(key_of[7], 1), REQUESTS // R_DEV)
    ids_turns = jax.random.permutation(jax.random.fold_in(key_of[7], 3), REQUESTS // R_DEV)
    ids = jax.vmap(lambda own, number: shared_out(jax.random.fold_in(key_of[7], 2), own, number, R_DEV, EXPERTS, TOP, CAP, 2))(ids_keys, ids_turns).reshape((REQUESTS, TOP))
    gates = jnp.clip(0.05 + 0.45 * jax.random.uniform(key_of[8], (REQUESTS, TOP), jnp.float32) ** levels(key_of[8], (REQUESTS, TOP), ((0, 128),), -0.2, 0.2), 0.05, 0.5)
    w_gate = gaussian(key_of[9], (EXPERTS * SLICES, D, HID_DEV), D ** -0.5, 0.0625, ((0, 128),))
    w_up = gaussian(key_of[10], (EXPERTS * SLICES, D, HID_DEV), D ** -0.5, 0.0625, ((0, 128),))
    w_down = gaussian(key_of[11], (EXPERTS * SLICES, HID_DEV, D), MOE_FF ** -0.5, 0.1875, ((0, 128),))
    return {"queries": queries, "cache": cache, "lengths": lengths, "w_uv": w_uv, "w_out": w_out, "residual": residual, "gain": gain, "ids": ids, "gates": gates, "w_gate": w_gate, "w_up": w_up, "w_down": w_down}


softmax_scale = 192.0 ** (-0.5)

def attend_one(args):
    query, kv, count = args
    score = jnp.dot(query, kv.T, preferred_element_type=jnp.float32) * softmax_scale
    live = jnp.arange(L_MAX, dtype=jnp.int32) < count
    score = jnp.where(live[None, :], score, -jnp.inf)
    peak = lax.optimization_barrier(jnp.max(score, axis=1, keepdims=True))
    weight = jnp.where(live[None, :], jnp.exp(score - peak), 0.0)
    total = lax.optimization_barrier(jnp.sum(weight, axis=1, keepdims=True))
    summed = jnp.dot(weight.astype(jnp.bfloat16), kv[:, :LATENT], preferred_element_type=jnp.float32)
    return (summed / total).astype(jnp.bfloat16)

def reference(queries, cache, lengths, w_uv, w_out, residual, gain, ids, gates, w_gate, w_up, w_down):
    latents = lax.map(attend_one, (queries, cache, lengths))
    values = jnp.einsum('rhc,hcv->rhv', latents.astype(jnp.float32), w_uv.astype(jnp.float32)).astype(jnp.bfloat16)
    attn = jnp.dot(values.reshape(REQUESTS, HEADS * VHEAD), w_out, preferred_element_type=jnp.float32)
    mixed = residual.astype(jnp.float32) + attn
    normed = (mixed * lax.rsqrt(lax.optimization_barrier(jnp.mean(mixed * mixed, axis=-1, keepdims=True)) + 1e-06) * gain).astype(jnp.bfloat16)
    pairs = ids.reshape(DEVICES, R_DEV * TOP)
    onehot = (pairs[..., None] == jnp.arange(EXPERTS, dtype=jnp.int32)).astype(jnp.int32)
    slot = lax.optimization_barrier(jnp.sum((jnp.cumsum(onehot, axis=1) - 1) * onehot, axis=-1)).astype(jnp.int32)
    source = jnp.broadcast_to(jnp.arange(DEVICES, dtype=jnp.int32)[:, None], pairs.shape)
    row_index = source * R_DEV + jnp.arange(R_DEV * TOP, dtype=jnp.int32)[None, :] // TOP
    table = jnp.full((EXPERTS, DEVICES, CAP), REQUESTS, jnp.int32).at[pairs, source, slot].set(row_index)
    padded = jnp.concatenate([normed, jnp.zeros((1, D), jnp.bfloat16)], axis=0)

    def expert(args):
        rows_idx, gate_blocks, up_blocks, down_blocks = args
        rows = padded[rows_idx.reshape(-1)]
        gate_mat = gate_blocks.transpose(1, 0, 2).reshape(D, MOE_FF)
        up_mat = up_blocks.transpose(1, 0, 2).reshape(D, MOE_FF)
        gate_val = jnp.dot(rows, gate_mat, preferred_element_type=jnp.float32)
        up_val = jnp.dot(rows, up_mat, preferred_element_type=jnp.float32)
        hidden = (jax.nn.silu(gate_val) * up_val).astype(jnp.bfloat16)
        result = jnp.dot(hidden, down_blocks.reshape(MOE_FF, D), preferred_element_type=jnp.float32)
        return result.reshape(DEVICES, CAP, D)
    outputs = lax.map(expert, (table, w_gate.reshape(EXPERTS, SLICES, D, HID_DEV), w_up.reshape(EXPERTS, SLICES, D, HID_DEV), w_down.reshape(EXPERTS, SLICES, HID_DEV, D)))
    picked = outputs[pairs, source, slot].reshape(REQUESTS, TOP, D)
    moe = lax.optimization_barrier(jnp.sum(picked * gates[..., None], axis=1))
    return (mixed + moe).astype(jnp.bfloat16)
```

```python
import functools

import jax
import jax.numpy as jnp
from jax import lax
from jax.experimental import pallas as pl
from jax.experimental.pallas import tpu as pltpu
from jax.sharding import PartitionSpec as P

LATENT = 512
VHEAD = 128
TOP = 8
AXES = ("grp", "dev")
F32 = jnp.float32
BF16 = jnp.bfloat16
I32 = jnp.int32
MIB = 1 << 20
CHUNK = 1024

softmax_scale = 192.0 ** (-0.5)


def device(y, z, x, c):
    return ((y * 4 + z) * 4 + x) * 2 + c


RINGS = [[device(y, z, x, 0) for x in range(4)] for y in range(4) for z in range(4)] + [
    [device(y, z, x, 1) for z in range(4)] for y in range(4) for x in range(4)
]
PLANES = [[device(y, z, x, 0) for y in range(4) for z in range(4)] for x in range(4)] + [
    [device(y, z, x, 1) for y in range(4) for x in range(4)] for z in range(4)
]
SIBLING = [(i, i ^ 1) for i in range(128)]


def swap(a):
    return lax.ppermute(a, AXES, SIBLING)


def ahead(a, step):
    return lax.ppermute(a, AXES, [(r[i], r[(i + step) % 4]) for r in RINGS for i in range(4)])


def plane(a):
    return lax.all_to_all(a, AXES, 0, 0, axis_index_groups=PLANES, tiled=True)


def exchange(blocks):
    return [blocks[0]] + [ahead(blocks[4 - j], 4 - j) for j in range(1, 4)]


def iota(shape, axis):
    return lax.broadcasted_iota(I32, shape, axis)


def pick(index, count):
    return jnp.where(index == iota((index.shape[0], count), 1), 1.0, 0.0).astype(BF16)


def coordinates():
    me = lax.axis_index("grp") * 64 + lax.axis_index("dev")
    core, z, x = me & 1, (me >> 3) & 3, (me >> 1) & 3
    return core, me >> 2, jnp.where(core == 0, x, z), jnp.where(core == 0, z, x)


HBM = pl.BlockSpec(memory_space=pltpu.HBM)
VMEM = pl.BlockSpec(memory_space=pltpu.VMEM)


def attend_kernel(
    lens, query, kv, w_out, sent, out_other, heads, peak, total, acc, both, held, sems
):
    r, j = pl.program_id(0), pl.program_id(1)
    step = r * pl.num_programs(1) + j
    core, _, me_t, _ = coordinates()
    half = held.shape[1]
    away = pl.ds(pl.multiple_of((1 - core) * half, 128), half)
    take = pltpu.make_async_copy(w_out.at[:, away], held, sems.at[0])
    give = pltpu.make_async_copy(held, out_other, sems.at[1])

    @pl.when(step == 0)
    def _():
        take.start()

    @pl.when(step == 1)
    def _():
        take.wait()
        give.start()

    @pl.when(j == 0)
    def _():
        i = iota((128, 1), 0)
        turned = lax.dot_general(
            pick(i, 128), query[0], (((1,), (1,)), ((), ())), preferred_element_type=F32
        )
        heads[...] = turned.astype(BF16)
        peak[...] = jnp.full_like(peak, -1e30)
        total[...] = jnp.zeros_like(total)
        acc[...] = jnp.zeros_like(acc)

    @pl.when(j * CHUNK < lens[r])
    def _():
        score = jnp.dot(heads[...], kv[0], preferred_element_type=F32)
        place = j * CHUNK + iota(score.shape, 1)
        score = jnp.where(place < lens[r], score * softmax_scale, -1e30)
        before = peak[...]
        now = jnp.maximum(before, jnp.max(score, axis=1, keepdims=True))
        fade = jnp.exp(before - now)
        weight = jnp.exp(score - now)
        peak[...] = now
        total[...] = total[...] * fade + jnp.sum(weight, axis=1, keepdims=True)
        acc[...] = acc[...] * fade + lax.dot_general(
            weight.astype(BF16),
            kv[0, :LATENT, :],
            (((1,), (1,)), ((), ())),
            preferred_element_type=F32,
        )

    @pl.when(j == pl.num_programs(1) - 1)
    def _():
        both[pl.ds(pl.multiple_of(r * 128, 128), 128), :] = (acc[...] / total[...]).astype(BF16)

    @pl.when(step == 2 * pl.num_programs(1) - 1)
    def _():
        i = iota((256, 1), 0)
        y, b, t = i >> 6, (i >> 4) & 3, (me_t + (i >> 2)) & 3
        z = jnp.where(core == 0, b, t)
        x = jnp.where(core == 0, t, b)
        head = device(y, z, x, ((i >> 1) & 1) ^ core)
        rows = jnp.dot(pick((i & 1) * 128 + head, 256), both[...], preferred_element_type=F32)
        sent[...] = rows.astype(BF16).reshape(sent.shape)
        give.wait()


def attend(lengths, queries, cache, w_out):
    _, size, heads = queries.shape
    half = w_out.shape[1] // 2
    chunks = cache.shape[2] // CHUNK

    def live(r, j, lens):
        return (r, 0, jnp.minimum(j, (lens[r] - 1) // CHUNK))

    return pl.pallas_call(
        attend_kernel,
        grid_spec=pltpu.PrefetchScalarGridSpec(
            num_scalar_prefetch=1,
            grid=(2, chunks),
            in_specs=[
                pl.BlockSpec((1, size, heads), lambda r, j, lens: (r, 0, 0)),
                pl.BlockSpec((1, size, CHUNK), live),
                HBM,
            ],
            out_specs=[
                pl.BlockSpec((16, 16, LATENT), lambda r, j, lens: (0, 0, 0)),
                HBM,
            ],
            scratch_shapes=[
                pltpu.VMEM((heads, size), BF16),
                pltpu.VMEM((heads, 1), F32),
                pltpu.VMEM((heads, 1), F32),
                pltpu.VMEM((heads, LATENT), F32),
                pltpu.VMEM((2 * heads, LATENT), BF16),
                pltpu.VMEM((VHEAD, half), BF16),
                pltpu.SemaphoreType.DMA((2,)),
            ],
        ),
        out_shape=[
            pltpu.VMEM((16, 16, LATENT), BF16),
            jax.ShapeDtypeStruct((VHEAD, half), BF16),
        ],
        compiler_params=pltpu.CompilerParams(vmem_limit_bytes=56 * MIB),
        name="attend",
    )(lengths, queries, cache, w_out)


def load_kernel(places, *refs):
    arrays, (out, sems) = refs[: len(places)], refs[len(places) :]
    core = coordinates()[0]
    copies = []
    for n, (array, (axis, rows, columns)) in enumerate(zip(arrays, places)):
        if axis == 0:
            start = pl.multiple_of(core * out.shape[0], 128)
            array = array.at[pl.ds(start, out.shape[0]), :]
        if axis == 1:
            start = pl.multiple_of(core * out.shape[1], 128)
            array = array.at[:, pl.ds(start, out.shape[1])]
        copies.append(pltpu.make_async_copy(array, out.at[rows, columns], sems.at[n]))
    for copy in copies:
        copy.start()
    for copy in copies:
        copy.wait()


def load(arrays, places, shape, name, limit):
    size = 2 * shape[0] * shape[1]
    return pl.pallas_call(
        functools.partial(load_kernel, places),
        in_specs=[HBM] * len(arrays),
        out_specs=VMEM,
        out_shape=pltpu.VMEM(shape, BF16),
        scratch_shapes=[pltpu.SemaphoreType.DMA((len(arrays),))],
        compiler_params=pltpu.CompilerParams(vmem_limit_bytes=limit * MIB),
        cost_estimate=pl.CostEstimate(flops=0, bytes_accessed=2 * size, transcendentals=0),
        name=name,
    )(*arrays)


def pack_kernel(gate, up, down, after, gate_out, up_out, down_out, mark, *scratch):
    held, sems = scratch[:3], scratch[3]
    core = coordinates()[0]
    half = down_out.shape[1]
    away = pl.ds(pl.multiple_of((1 - core) * half, 128), half)
    sources = (gate.at[away, :], up.at[away, :], down.at[:, away])
    outs = (gate_out, up_out, down_out)
    takes = [pltpu.make_async_copy(a, b, sems.at[n]) for n, (a, b) in enumerate(zip(sources, held))]
    gives = [pltpu.make_async_copy(a, b, sems.at[3 + n]) for n, (a, b) in enumerate(zip(held, outs))]
    for take in takes:
        take.start()
    mark[...] = jnp.zeros_like(mark)
    for take, give in zip(takes, gives):
        take.wait()
        give.start()
    for give in gives:
        give.wait()


def pack(gate, up, down, after):
    half = down.shape[1] // 2
    shapes = [(half, 256), (half, 256), (256, half)]
    return pl.pallas_call(
        pack_kernel,
        in_specs=[HBM] * 3 + [pl.BlockSpec(memory_space=pl.ANY)],
        out_specs=[HBM] * 3 + [VMEM],
        out_shape=[jax.ShapeDtypeStruct(shape, BF16) for shape in shapes]
        + [pltpu.VMEM((8, 128), F32)],
        scratch_shapes=[pltpu.VMEM(shape, BF16) for shape in shapes]
        + [pltpu.SemaphoreType.DMA((6,))],
        compiler_params=pltpu.CompilerParams(vmem_limit_bytes=56 * MIB),
        cost_estimate=pl.CostEstimate(flops=0, bytes_accessed=12 * MIB, transcendentals=0),
        name="pack",
    )(gate, up, down, after)


def call(kernel, args, outs, name, flops, scratch=()):
    return pl.pallas_call(
        kernel,
        in_specs=[VMEM] * len(args),
        out_specs=[VMEM] * len(outs),
        out_shape=[jax.ShapeDtypeStruct(*out) for out in outs],
        scratch_shapes=list(scratch),
        compiler_params=pltpu.CompilerParams(vmem_limit_bytes=24 * MIB),
        cost_estimate=pl.CostEstimate(flops=flops, bytes_accessed=1 << 20, transcendentals=0),
        name=name,
    )(*args)


def turn_kernel(got, mark, o0, o1, o2, o3):
    rows = got[...].reshape(256, got.shape[2])
    i = iota((256, 1), 0)
    index = (i & 15) * 16 + (i >> 6) * 4 + ((i >> 4) & 3)
    rows = jnp.dot(pick(index, 256), rows, preferred_element_type=F32).astype(BF16)
    for d, out in enumerate((o0, o1, o2, o3)):
        out[...] = rows[d * 64 : d * 64 + 64]


def values_kernel(p0, p1, p2, p3, uv_own, uv_other, out):
    for head, uv in enumerate((uv_own, uv_other)):
        rows = jnp.concatenate(
            [p[head * 32 : head * 32 + 32, :] for p in (p0, p1, p2, p3)], axis=0
        )
        val = jnp.dot(rows, uv[...], preferred_element_type=F32)
        out[:, head * VHEAD : head * VHEAD + VHEAD] = val.astype(BF16)


PARTS = ((0, 64), (64, 96), (96, 128), (128, 160), (160, 192), (192, 224), (224, 256))


LATE = PARTS[:3] + PARTS[5:] + PARTS[3:5]


def put_parts(full, outs, columns, parts):
    for ref, (lo, hi) in zip(outs, parts):
        ref[:, columns] = full[lo:hi].astype(BF16)


def project_kernel(mine, theirs, w, *refs):
    outs, val = refs[:-1], refs[-1]
    _, _, me_t, me_p = coordinates()
    i = iota((128, 1), 0)
    t, b = ((i >> 5) + me_t) & 3, i & 3
    index = ((b - me_p) & 3) * 32 + (i & 0x1C) + t
    sib = jnp.dot(pick(index, 128), theirs[...], preferred_element_type=F32).astype(BF16)
    for d in range(4):
        for s, rows in enumerate((mine[...], sib)):
            at = d * 64 + s * 32
            rows = rows[d * 32 : d * 32 + 32]
            val[at : at + 32, s * VHEAD : s * VHEAD + VHEAD] = rows[:, :VHEAD]
            val[at : at + 32, (1 - s) * VHEAD : (2 - s) * VHEAD] = rows[:, VHEAD:]
    quarter = w.shape[1] // 4
    for q in range(4):
        columns = slice(q * quarter, (q + 1) * quarter)
        full = jnp.dot(val[...], w[:, columns], preferred_element_type=F32)
        put_parts(full, outs, columns, PARTS)


def product_outs(half):
    return [((hi - lo, half), BF16) for lo, hi in PARTS]


def gate_up_kernel(first, *refs):
    before, refs = refs[: 4 if first else 0], refs[4 if first else 0 :]
    pieces, (back, w), outs = refs[:-6], refs[-6:-4], refs[-4:]
    for done, out in zip(before, outs):
        out[:first, :] = done[...]
    count = outs[0].shape[0] - first
    part, sent, squares, weight = (out.at[pl.ds(first, count), :] for out in outs)
    expert = coordinates()[1]
    half = w.shape[0]
    quarter = half // 4
    sq = jnp.zeros((count, 1), F32)
    for q in range(4):
        columns = slice(q * quarter, (q + 1) * quarter)
        a = jnp.concatenate([p[:, columns] for p in pieces], axis=0)
        share = jnp.dot(a, w[columns, :], preferred_element_type=F32)
        if q == 0:
            part[...] = share
        else:
            part[...] += share
        plain = a.astype(F32) * back[:, columns]
        sq += jnp.sum(plain * plain, axis=1, keepdims=True)
    squares[...] = sq
    sent[:, :1024] = part[...].astype(BF16)
    hi = sq.astype(BF16).astype(F32)
    mid = (sq - hi).astype(BF16).astype(F32)
    lo = sq - hi - mid
    lane = iota((count, 128), 1)
    sent[:, 1024:] = jnp.where(
        lane == 0, hi, jnp.where(lane == 1, mid, jnp.where(lane == 2, lo, 0.0))
    ).astype(BF16)
    n = jnp.concatenate([p[:, half:] for p in pieces], axis=0).astype(F32)
    high = pltpu.roll(n, 128 - TOP, 1)
    low = pltpu.roll(n, 128 - 2 * TOP, 1)
    hit = (lane < TOP) & (n == expert.astype(F32))
    weight[...] = jnp.sum(jnp.where(hit, high + low, 0.0), axis=1, keepdims=True)


def gate_up(before, pieces, back, w):
    first = before[0].shape[0] if before else 0
    fresh = sum(p.shape[0] for p in pieces)
    count = first + fresh
    return call(
        functools.partial(gate_up_kernel, first),
        (*before, *pieces, back, w),
        [((count, 1024), F32), ((count, 1152), BF16), ((count, 1), F32), ((count, 1), F32)],
        "gate_up",
        fresh << 23,
    )


def late(d):
    return d ^ (d >> 1)


def down_kernel(part, squares, got, weight, w, *refs):
    outs, hidden = refs[:-1], refs[-1]
    _, _, me_t, me_p = coordinates()
    i = iota((256, 1), 0)
    d, s, rest = late(i >> 6), (i >> 5) & 1, i & 0x1C
    t, b = (d + me_t) & 3, i & 3
    index = late((b - me_p) & 3) * 64 + (1 - s) * 32 + rest + t
    theirs = jnp.dot(pick(index, 256), got[...], preferred_element_type=F32)
    tail = theirs[:, 1024:]
    lane = iota(tail.shape, 1)
    sq = squares[...] + jnp.sum(jnp.where(lane < 3, tail, 0.0), axis=1, keepdims=True)
    scale = lax.rsqrt(sq / 7168.0 + 1e-06)
    for block in range(2):
        at, back = block * 512, 512 - block * 512
        gate = (part[:, at : at + 256] + theirs[:, back : back + 256]) * scale
        up = (part[:, at + 256 : at + 512] + theirs[:, back + 256 : back + 512]) * scale
        hidden[:, block * 256 : block * 256 + 256] = (
            gate / (1.0 + jnp.exp(-gate)) * up
        ).astype(BF16)
    quarter = w.shape[1] // 4
    for q in range(4):
        columns = slice(q * quarter, (q + 1) * quarter)
        full = jnp.dot(hidden[...], w[:, columns], preferred_element_type=F32)
        put_parts(full * weight[...], outs, columns, LATE)


def add(a, b):
    return (a.astype(F32) + b.astype(F32)).astype(BF16)


def reduce_rows(b0, b1t, b1b, b2t, b2b, b3t, b3b):
    far_left, far_right = ahead(b2t, 1), ahead(b2b, -1)
    left_b, right_t = ahead(b1b, 1), ahead(b3t, -1)
    left_t, right_b = ahead(add(b1t, far_left), 1), ahead(add(b3b, far_right), -1)
    left = jnp.concatenate([left_t, left_b])
    right = jnp.concatenate([right_t, right_b])
    mine = (b0.astype(F32) + left.astype(F32) + right.astype(F32)).astype(BF16)
    mine = mine.reshape(4, 16, mine.shape[1]).swapaxes(0, 1)
    return jnp.sum(plane(mine).astype(F32), axis=0)


def gather_rows(a):
    a0 = plane(jnp.broadcast_to(a, (16, *a.shape)))
    a0 = a0.swapaxes(0, 1).reshape(64, a.shape[1])
    top, bottom = a0[:32], a0[32:]
    left_t, right_b = ahead(top, 1), ahead(bottom, -1)
    left_b, right_t = ahead(bottom, 1), ahead(top, -1)
    return (a0, right_t, right_b, left_t, left_b), (ahead(left_t, 1), ahead(right_b, -1))


def shards(queries, cache, lengths, w_uv, w_out, residual, gain, ids, gates, w_gate, w_up, w_down):
    core = lax.axis_index(AXES) % 2
    half = residual.shape[1] // 2

    def own(w, axis):
        return lax.dynamic_slice_in_dim(w, core * half, half, axis)

    def away(w, axis):
        return lax.dynamic_slice_in_dim(w, (1 - core) * half, half, axis)

    sent, out_other = attend(lengths, queries.swapaxes(1, 2), cache.swapaxes(1, 2), w_out)
    uv_other = swap(w_uv[0])
    *packed, mark = pack(w_gate[0], w_up[0], w_down[0], out_other)
    blocks = pl.pallas_call(
        turn_kernel,
        in_specs=[VMEM, VMEM],
        out_specs=[VMEM] * 4,
        out_shape=[jax.ShapeDtypeStruct((64, LATENT), BF16)] * 4,
        compiler_params=pltpu.CompilerParams(vmem_limit_bytes=16 * MIB),
        name="turn",
    )(plane(sent), mark)
    blocks = exchange(blocks)
    out_other = swap(out_other)
    every = slice(None)
    w_out = load(
        (w_out, out_other),
        ((1, slice(0, VHEAD), every), (None, slice(VHEAD, 2 * VHEAD), every)),
        (2 * VHEAD, half),
        "load_out",
        8,
    )
    (mine,) = call(
        values_kernel,
        (*blocks, w_uv[0], uv_other),
        [((128, 2 * VHEAD), BF16)],
        "values",
        1 << 25,
    )
    gate_other, up_other, down_other = (swap(a) for a in packed)

    gates_hi = gates.astype(BF16)
    gates_lo = (gates - gates_hi.astype(F32)).astype(BF16)
    names = jnp.concatenate(
        [ids.astype(BF16), gates_hi, gates_lo, jnp.zeros((2, 128 - 3 * TOP), BF16)], axis=1
    )
    rows = jnp.concatenate(
        [
            jnp.concatenate([own(residual, 1), names], axis=1),
            swap(jnp.concatenate([away(residual, 1), names], axis=1)),
        ]
    )
    res, names = rows[:, :half].astype(F32), rows[:, half:]

    pieces = call(
        project_kernel,
        (mine, swap(mine), w_out),
        product_outs(half),
        "project",
        1 << 29,
        [pltpu.VMEM((256, 2 * VHEAD), BF16)],
    )
    mixed = res + reduce_rows(*pieces)

    scaled = (mixed * own(gain, 0)).astype(BF16)
    w_gu = load(
        (w_gate[0], w_up[0], gate_other, up_other),
        tuple((0 if n < 2 else None, every, slice(256 * n, 256 * n + 256)) for n in range(4)),
        (half, 1024),
        "load_gate_up",
        42,
    )
    near, far = gather_rows(jnp.concatenate([scaled, names], axis=1))
    back = (1.0 / own(gain, 0)).reshape(1, half)
    before = gate_up((), near, back, w_gu)
    part, sent, squares, weight = gate_up(before, far, back, w_gu)
    w_down = load(
        (w_down[0], down_other),
        ((1, slice(0, 256), every), (None, slice(256, 512), every)),
        (512, half),
        "load_down",
        46,
    )
    pieces = call(
        down_kernel,
        (part, squares, swap(sent), weight, w_down),
        product_outs(half),
        "down",
        1 << 30,
        [pltpu.VMEM((256, 512), BF16)],
    )
    result = (mixed + reduce_rows(*pieces)).astype(BF16)

    mine, other = result[:2], swap(result[2:])
    return jnp.where(
        core == 0, jnp.concatenate([mine, other], 1), jnp.concatenate([other, mine], 1)
    )


def solution(mesh):
    in_specs = (
        P(("grp", "dev"), None, None),
        P(("grp", "dev"), None, None),
        P(("grp", "dev")),
        P(("grp", "dev"), None, None),
        P(("grp", "dev"), None),
        P(("grp", "dev"), None),
        P(),
        P(("grp", "dev"), None),
        P(("grp", "dev"), None),
        P(("grp", "dev"), None, None),
        P(("grp", "dev"), None, None),
        P(("grp", "dev"), None, None),
    )
    out_specs = P(("grp", "dev"), None)
    return jax.shard_map(shards, mesh=mesh, in_specs=in_specs, out_specs=out_specs, check_vma=False)
```

```python
import functools

import jax
import jax.numpy as jnp
from jax import lax
from jax.experimental import pallas as pl
from jax.experimental.pallas import tpu as pltpu
from jax.sharding import PartitionSpec as P

LATENT = 512
VHEAD = 128
TOP = 8
AXES = ("grp", "dev")
F32 = jnp.float32
BF16 = jnp.bfloat16
I32 = jnp.int32
MIB = 1 << 20
CHUNK = 512

softmax_scale = 192.0 ** (-0.5)


def device(y, z, x, c):
    return ((y * 4 + z) * 4 + x) * 2 + (c ^ ((x + z) & 1))


RINGS = [[device(y, z, x, 0) for x in range(4)] for y in range(4) for z in range(4)] + [
    [device(y, z, x, 1) for z in range(4)] for y in range(4) for x in range(4)
]
PLANES = [[device(y, z, x, 0) for y in range(4) for z in range(4)] for x in range(4)] + [
    [device(y, z, x, 1) for y in range(4) for x in range(4)] for z in range(4)
]
SIBLING = [(i, i ^ 1) for i in range(128)]


def swap(a):
    return lax.ppermute(a, AXES, SIBLING)


def ahead(a, step):
    return lax.ppermute(a, AXES, [(r[i], r[(i + step) % 4]) for r in RINGS for i in range(4)])


def plane(a):
    return lax.all_to_all(a, AXES, 0, 0, axis_index_groups=PLANES, tiled=True)


def exchange(blocks):
    return [blocks[0]] + [ahead(blocks[4 - j], 4 - j) for j in range(1, 4)]


def iota(shape, axis):
    return lax.broadcasted_iota(I32, shape, axis)


def pick(index, count):
    return jnp.where(index == iota((index.shape[0], count), 1), 1.0, 0.0).astype(BF16)


def coordinates():
    me = lax.axis_index("grp") * 64 + lax.axis_index("dev")
    z, x = (me >> 3) & 3, (me >> 1) & 3
    core = (me ^ x ^ z) & 1
    return core, me >> 2, jnp.where(core == 0, x, z), jnp.where(core == 0, z, x)


HBM = pl.BlockSpec(memory_space=pltpu.HBM)
VMEM = pl.BlockSpec(memory_space=pltpu.VMEM)


def attend_kernel(
    lens, query, cache, w_out, sent, out_other, q, kv, peak, total, acc, both, held, sems, kv_sems
):
    core, _, me_t, _ = coordinates()
    half = held.shape[1]
    away = pl.ds(pl.multiple_of((1 - core) * half, 128), half)
    take = pltpu.make_async_copy(w_out.at[:, away], held, sems.at[0])
    give = pltpu.make_async_copy(held, out_other, sems.at[1])
    ask = pltpu.make_async_copy(query, q, sems.at[2])

    def chunk(r, j):
        slots = pl.ds(pl.multiple_of(j * CHUNK, CHUNK), CHUNK)
        return pltpu.make_async_copy(cache.at[r, :, slots], kv.at[r, j], kv_sems.at[r, j])

    live = [(lens[r] + CHUNK - 1) // CHUNK for r in range(2)]
    ask.start()
    for r in range(2):

        @pl.loop(0, live[r])
        def _(j, r=r):
            chunk(r, j).start()

    take.start()
    ask.wait()
    for r in range(2):
        heads = lax.dot_general(
            pick(iota((128, 1), 0), 128), q[r], (((1,), (1,)), ((), ())), preferred_element_type=F32
        ).astype(BF16)
        peak[...] = jnp.full_like(peak, -1e30)
        total[...] = jnp.zeros_like(total)
        acc[...] = jnp.zeros_like(acc)

        @pl.loop(0, live[r])
        def _(j, r=r, heads=heads):
            chunk(r, j).wait()
            score = jnp.dot(heads, kv[r, j], preferred_element_type=F32)
            place = j * CHUNK + iota(score.shape, 1)
            score = jnp.where(place < lens[r], score * softmax_scale, -1e30)
            before = peak[...]
            now = jnp.maximum(before, jnp.max(score, axis=1, keepdims=True))
            fade = jnp.exp(before - now)
            weight = jnp.exp(score - now)
            peak[...] = now
            total[...] = total[...] * fade + jnp.sum(weight, axis=1, keepdims=True)
            acc[...] = acc[...] * fade + lax.dot_general(
                weight.astype(BF16),
                kv[r, j, :LATENT, :],
                (((1,), (1,)), ((), ())),
                preferred_element_type=F32,
            )

        both[r * 128 : r * 128 + 128, :] = (acc[...] / total[...]).astype(BF16)
        if r == 0:
            take.wait()
            give.start()

    i = iota((256, 1), 0)
    y, b, t = i >> 6, (i >> 4) & 3, (me_t + (i >> 2)) & 3
    z = jnp.where(core == 0, b, t)
    x = jnp.where(core == 0, t, b)
    head = device(y, z, x, ((i >> 1) & 1) ^ core)
    rows = jnp.dot(pick((i & 1) * 128 + head, 256), both[...], preferred_element_type=F32)
    sent[...] = rows.astype(BF16).reshape(sent.shape)
    give.wait()


def attend(lengths, queries, cache, w_out):
    _, size, heads = queries.shape
    half = w_out.shape[1] // 2
    chunks = cache.shape[2] // CHUNK
    return pl.pallas_call(
        attend_kernel,
        in_specs=[pl.BlockSpec(memory_space=pltpu.SMEM), HBM, HBM, HBM],
        out_specs=[VMEM, HBM],
        out_shape=[
            pltpu.VMEM((16, 16, LATENT), BF16),
            jax.ShapeDtypeStruct((VHEAD, half), BF16),
        ],
        scratch_shapes=[
            pltpu.VMEM((2, size, heads), BF16),
            pltpu.VMEM((2, chunks, size, CHUNK), BF16),
            pltpu.VMEM((heads, 1), F32),
            pltpu.VMEM((heads, 1), F32),
            pltpu.VMEM((heads, LATENT), F32),
            pltpu.VMEM((2 * heads, LATENT), BF16),
            pltpu.VMEM((VHEAD, half), BF16),
            pltpu.SemaphoreType.DMA((3,)),
            pltpu.SemaphoreType.DMA((2, chunks)),
        ],
        compiler_params=pltpu.CompilerParams(vmem_limit_bytes=56 * MIB),
        name="attend",
    )(lengths, queries, cache, w_out)


def load_kernel(places, *refs):
    arrays, (out, sems) = refs[: len(places)], refs[len(places) :]
    core = coordinates()[0]
    copies = []
    for n, (array, (axis, rows, columns)) in enumerate(zip(arrays, places)):
        if axis == 0:
            start = pl.multiple_of(core * out.shape[0], 128)
            array = array.at[pl.ds(start, out.shape[0]), :]
        if axis == 1:
            start = pl.multiple_of(core * out.shape[1], 128)
            array = array.at[:, pl.ds(start, out.shape[1])]
        copies.append(pltpu.make_async_copy(array, out.at[rows, columns], sems.at[n]))
    for copy in copies:
        copy.start()
    for copy in copies:
        copy.wait()


def load(arrays, places, shape, name, limit):
    size = 2 * shape[0] * shape[1]
    return pl.pallas_call(
        functools.partial(load_kernel, places),
        in_specs=[HBM] * len(arrays),
        out_specs=VMEM,
        out_shape=pltpu.VMEM(shape, BF16),
        scratch_shapes=[pltpu.SemaphoreType.DMA((len(arrays),))],
        compiler_params=pltpu.CompilerParams(vmem_limit_bytes=limit * MIB),
        cost_estimate=pl.CostEstimate(flops=0, bytes_accessed=2 * size, transcendentals=0),
        name=name,
    )(*arrays)


def pack_kernel(gate, up, down, after, gate_out, up_out, down_out, mark, *scratch):
    held, sems = scratch[:3], scratch[3]
    core = coordinates()[0]
    half = down_out.shape[1]
    away = pl.ds(pl.multiple_of((1 - core) * half, 128), half)
    sources = (gate.at[away, :], up.at[away, :], down.at[:, away])
    outs = (gate_out, up_out, down_out)
    takes = [pltpu.make_async_copy(a, b, sems.at[n]) for n, (a, b) in enumerate(zip(sources, held))]
    gives = [pltpu.make_async_copy(a, b, sems.at[3 + n]) for n, (a, b) in enumerate(zip(held, outs))]
    for take in takes:
        take.start()
    mark[...] = jnp.zeros_like(mark)
    for take, give in zip(takes, gives):
        take.wait()
        give.start()
    for give in gives:
        give.wait()


def pack(gate, up, down, after):
    half = down.shape[1] // 2
    shapes = [(half, 256), (half, 256), (256, half)]
    return pl.pallas_call(
        pack_kernel,
        in_specs=[HBM] * 3 + [pl.BlockSpec(memory_space=pl.ANY)],
        out_specs=[HBM] * 3 + [VMEM],
        out_shape=[jax.ShapeDtypeStruct(shape, BF16) for shape in shapes]
        + [pltpu.VMEM((8, 128), F32)],
        scratch_shapes=[pltpu.VMEM(shape, BF16) for shape in shapes]
        + [pltpu.SemaphoreType.DMA((6,))],
        compiler_params=pltpu.CompilerParams(vmem_limit_bytes=56 * MIB),
        cost_estimate=pl.CostEstimate(flops=0, bytes_accessed=12 * MIB, transcendentals=0),
        name="pack",
    )(gate, up, down, after)


def call(kernel, args, outs, name, flops, scratch=()):
    return pl.pallas_call(
        kernel,
        in_specs=[VMEM] * len(args),
        out_specs=[VMEM] * len(outs),
        out_shape=[jax.ShapeDtypeStruct(*out) for out in outs],
        scratch_shapes=list(scratch),
        compiler_params=pltpu.CompilerParams(vmem_limit_bytes=24 * MIB),
        cost_estimate=pl.CostEstimate(flops=flops, bytes_accessed=1 << 20, transcendentals=0),
        name=name,
    )(*args)


def turn_kernel(got, mark, o0, o1, o2, o3):
    rows = got[...].reshape(256, got.shape[2])
    i = iota((256, 1), 0)
    index = (i & 15) * 16 + (i >> 6) * 4 + ((i >> 4) & 3)
    rows = jnp.dot(pick(index, 256), rows, preferred_element_type=F32).astype(BF16)
    for d, out in enumerate((o0, o1, o2, o3)):
        out[...] = rows[d * 64 : d * 64 + 64]


def values_kernel(p0, p1, p2, p3, uv_own, uv_other, out):
    for head, uv in enumerate((uv_own, uv_other)):
        rows = jnp.concatenate(
            [p[head * 32 : head * 32 + 32, :] for p in (p0, p1, p2, p3)], axis=0
        )
        val = jnp.dot(rows, uv[...], preferred_element_type=F32)
        out[:, head * VHEAD : head * VHEAD + VHEAD] = val.astype(BF16)


PARTS = ((0, 64), (64, 96), (96, 128), (128, 160), (160, 192), (192, 224), (224, 256))


LATE = PARTS[:3] + PARTS[5:] + PARTS[3:5]


def put_parts(full, outs, columns, parts):
    for ref, (lo, hi) in zip(outs, parts):
        ref[:, columns] = full[lo:hi].astype(BF16)


def project_kernel(mine, theirs, w, *refs):
    outs, val = refs[:-1], refs[-1]
    _, _, me_t, me_p = coordinates()
    i = iota((128, 1), 0)
    t, b = ((i >> 5) + me_t) & 3, i & 3
    index = ((b - me_p) & 3) * 32 + (i & 0x1C) + t
    sib = jnp.dot(pick(index, 128), theirs[...], preferred_element_type=F32).astype(BF16)
    for d in range(4):
        for s, rows in enumerate((mine[...], sib)):
            at = d * 64 + s * 32
            rows = rows[d * 32 : d * 32 + 32]
            val[at : at + 32, s * VHEAD : s * VHEAD + VHEAD] = rows[:, :VHEAD]
            val[at : at + 32, (1 - s) * VHEAD : (2 - s) * VHEAD] = rows[:, VHEAD:]
    quarter = w.shape[1] // 4
    for q in range(4):
        columns = slice(q * quarter, (q + 1) * quarter)
        full = jnp.dot(val[...], w[:, columns], preferred_element_type=F32)
        put_parts(full, outs, columns, PARTS)


def product_outs(half):
    return [((hi - lo, half), BF16) for lo, hi in PARTS]


def gate_up_kernel(first, *refs):
    before, refs = refs[: 4 if first else 0], refs[4 if first else 0 :]
    pieces, (back, w), outs = refs[:-6], refs[-6:-4], refs[-4:]
    for done, out in zip(before, outs):
        out[:first, :] = done[...]
    count = outs[0].shape[0] - first
    part, sent, squares, weight = (out.at[pl.ds(first, count), :] for out in outs)
    expert = coordinates()[1]
    half = w.shape[0]
    quarter = half // 4
    sq = jnp.zeros((count, 1), F32)
    for q in range(4):
        columns = slice(q * quarter, (q + 1) * quarter)
        a = jnp.concatenate([p[:, columns] for p in pieces], axis=0)
        share = jnp.dot(a, w[columns, :], preferred_element_type=F32)
        if q == 0:
            part[...] = share
        else:
            part[...] += share
        plain = a.astype(F32) * back[:, columns]
        sq += jnp.sum(plain * plain, axis=1, keepdims=True)
    squares[...] = sq
    sent[:, :1024] = part[...].astype(BF16)
    hi = sq.astype(BF16).astype(F32)
    mid = (sq - hi).astype(BF16).astype(F32)
    lo = sq - hi - mid
    lane = iota((count, 128), 1)
    sent[:, 1024:] = jnp.where(
        lane == 0, hi, jnp.where(lane == 1, mid, jnp.where(lane == 2, lo, 0.0))
    ).astype(BF16)
    n = jnp.concatenate([p[:, half:] for p in pieces], axis=0).astype(F32)
    high = pltpu.roll(n, 128 - TOP, 1)
    low = pltpu.roll(n, 128 - 2 * TOP, 1)
    hit = (lane < TOP) & (n == expert.astype(F32))
    weight[...] = jnp.sum(jnp.where(hit, high + low, 0.0), axis=1, keepdims=True)


def gate_up(before, pieces, back, w):
    first = before[0].shape[0] if before else 0
    fresh = sum(p.shape[0] for p in pieces)
    count = first + fresh
    return call(
        functools.partial(gate_up_kernel, first),
        (*before, *pieces, back, w),
        [((count, 1024), F32), ((count, 1152), BF16), ((count, 1), F32), ((count, 1), F32)],
        "gate_up",
        fresh << 23,
    )


def late(d):
    return d ^ (d >> 1)


def down_kernel(part, squares, got, weight, w, *refs):
    outs, hidden = refs[:-1], refs[-1]
    _, _, me_t, me_p = coordinates()
    i = iota((256, 1), 0)
    d, s, rest = late(i >> 6), (i >> 5) & 1, i & 0x1C
    t, b = (d + me_t) & 3, i & 3
    index = late((b - me_p) & 3) * 64 + (1 - s) * 32 + rest + t
    theirs = jnp.dot(pick(index, 256), got[...], preferred_element_type=F32)
    tail = theirs[:, 1024:]
    lane = iota(tail.shape, 1)
    sq = squares[...] + jnp.sum(jnp.where(lane < 3, tail, 0.0), axis=1, keepdims=True)
    scale = lax.rsqrt(sq / 7168.0 + 1e-06)
    for block in range(2):
        at, back = block * 512, 512 - block * 512
        gate = (part[:, at : at + 256] + theirs[:, back : back + 256]) * scale
        up = (part[:, at + 256 : at + 512] + theirs[:, back + 256 : back + 512]) * scale
        hidden[:, block * 256 : block * 256 + 256] = (
            gate / (1.0 + jnp.exp(-gate)) * up
        ).astype(BF16)
    quarter = w.shape[1] // 4
    for q in range(4):
        columns = slice(q * quarter, (q + 1) * quarter)
        full = jnp.dot(hidden[...], w[:, columns], preferred_element_type=F32)
        put_parts(full * weight[...], outs, columns, LATE)


def add(a, b):
    return (a.astype(F32) + b.astype(F32)).astype(BF16)


def reduce_rows(b0, b1t, b1b, b2t, b2b, b3t, b3b):
    far_left, far_right = ahead(b2t, 1), ahead(b2b, -1)
    left_b, right_t = ahead(b1b, 1), ahead(b3t, -1)
    left_t, right_b = ahead(add(b1t, far_left), 1), ahead(add(b3b, far_right), -1)
    left = jnp.concatenate([left_t, left_b])
    right = jnp.concatenate([right_t, right_b])
    mine = (b0.astype(F32) + left.astype(F32) + right.astype(F32)).astype(BF16)
    mine = mine.reshape(4, 16, mine.shape[1]).swapaxes(0, 1)
    return jnp.sum(plane(mine).astype(F32), axis=0)


def gather_rows(a):
    a0 = plane(jnp.broadcast_to(a, (16, *a.shape)))
    a0 = a0.swapaxes(0, 1).reshape(64, a.shape[1])
    top, bottom = a0[:32], a0[32:]
    left_t, right_b = ahead(top, 1), ahead(bottom, -1)
    left_b, right_t = ahead(bottom, 1), ahead(top, -1)
    return (a0, right_t, right_b, left_t, left_b), (ahead(left_t, 1), ahead(right_b, -1))


def shards(queries, cache, lengths, w_uv, w_out, residual, gain, ids, gates, w_gate, w_up, w_down):
    me = lax.axis_index(AXES)
    core = (me ^ (me >> 1) ^ (me >> 3)) & 1
    half = residual.shape[1] // 2

    def own(w, axis):
        return lax.dynamic_slice_in_dim(w, core * half, half, axis)

    def away(w, axis):
        return lax.dynamic_slice_in_dim(w, (1 - core) * half, half, axis)

    sent, out_other = attend(lengths, queries.swapaxes(1, 2), cache.swapaxes(1, 2), w_out)
    uv_other = swap(w_uv[0])
    *packed, mark = pack(w_gate[0], w_up[0], w_down[0], out_other)
    blocks = pl.pallas_call(
        turn_kernel,
        in_specs=[VMEM, VMEM],
        out_specs=[VMEM] * 4,
        out_shape=[jax.ShapeDtypeStruct((64, LATENT), BF16)] * 4,
        compiler_params=pltpu.CompilerParams(vmem_limit_bytes=16 * MIB),
        name="turn",
    )(plane(sent), mark)
    blocks = exchange(blocks)
    out_other = swap(out_other)
    every = slice(None)
    w_out = load(
        (w_out, out_other),
        ((1, slice(0, VHEAD), every), (None, slice(VHEAD, 2 * VHEAD), every)),
        (2 * VHEAD, half),
        "load_out",
        8,
    )
    (mine,) = call(
        values_kernel,
        (*blocks, w_uv[0], uv_other),
        [((128, 2 * VHEAD), BF16)],
        "values",
        1 << 25,
    )
    gate_other, up_other, down_other = (swap(a) for a in packed)

    gates_hi = gates.astype(BF16)
    gates_lo = (gates - gates_hi.astype(F32)).astype(BF16)
    names = jnp.concatenate(
        [ids.astype(BF16), gates_hi, gates_lo, jnp.zeros((2, 128 - 3 * TOP), BF16)], axis=1
    )
    rows = jnp.concatenate(
        [
            jnp.concatenate([own(residual, 1), names], axis=1),
            swap(jnp.concatenate([away(residual, 1), names], axis=1)),
        ]
    )
    res, names = rows[:, :half].astype(F32), rows[:, half:]

    pieces = call(
        project_kernel,
        (mine, swap(mine), w_out),
        product_outs(half),
        "project",
        1 << 29,
        [pltpu.VMEM((256, 2 * VHEAD), BF16)],
    )
    mixed = res + reduce_rows(*pieces)

    scaled = (mixed * own(gain, 0)).astype(BF16)
    w_gu = load(
        (w_gate[0], w_up[0], gate_other, up_other),
        tuple((0 if n < 2 else None, every, slice(256 * n, 256 * n + 256)) for n in range(4)),
        (half, 1024),
        "load_gate_up",
        42,
    )
    near, far = gather_rows(jnp.concatenate([scaled, names], axis=1))
    back = (1.0 / own(gain, 0)).reshape(1, half)
    before = gate_up((), near, back, w_gu)
    part, sent, squares, weight = gate_up(before, far, back, w_gu)
    w_down = load(
        (w_down[0], down_other),
        ((1, slice(0, 256), every), (None, slice(256, 512), every)),
        (512, half),
        "load_down",
        46,
    )
    pieces = call(
        down_kernel,
        (part, squares, swap(sent), weight, w_down),
        product_outs(half),
        "down",
        1 << 30,
        [pltpu.VMEM((256, 512), BF16)],
    )
    result = (mixed + reduce_rows(*pieces)).astype(BF16)

    mine, other = result[:2], swap(result[2:])
    return jnp.where(
        core == 0, jnp.concatenate([mine, other], 1), jnp.concatenate([other, mine], 1)
    )


def solution(mesh):
    in_specs = (
        P(("grp", "dev"), None, None),
        P(("grp", "dev"), None, None),
        P(("grp", "dev")),
        P(("grp", "dev"), None, None),
        P(("grp", "dev"), None),
        P(("grp", "dev"), None),
        P(),
        P(("grp", "dev"), None),
        P(("grp", "dev"), None),
        P(("grp", "dev"), None, None),
        P(("grp", "dev"), None, None),
        P(("grp", "dev"), None, None),
    )
    out_specs = P(("grp", "dev"), None)
    return jax.shard_map(shards, mesh=mesh, in_specs=in_specs, out_specs=out_specs, check_vma=False)
```

```python
import functools

import jax
import jax.numpy as jnp
from jax import lax
from jax.experimental import pallas as pl
from jax.experimental.pallas import tpu as pltpu
from jax.sharding import PartitionSpec as P

LATENT = 512
VHEAD = 128
TOP = 8
AXES = ("grp", "dev")
F32 = jnp.float32
BF16 = jnp.bfloat16
I32 = jnp.int32
MIB = 1 << 20
CHUNK = 1024

softmax_scale = 192.0 ** (-0.5)


def device(y, z, x, c):
    return ((y * 4 + z) * 4 + x) * 2 + (c ^ ((x + z) & 1))


RINGS = [[device(y, z, x, 0) for x in range(4)] for y in range(4) for z in range(4)] + [
    [device(y, z, x, 1) for z in range(4)] for y in range(4) for x in range(4)
]
PLANES = [[device(y, z, x, 0) for y in range(4) for z in range(4)] for x in range(4)] + [
    [device(y, z, x, 1) for y in range(4) for x in range(4)] for z in range(4)
]
SIBLING = [(i, i ^ 1) for i in range(128)]


def swap(a):
    return lax.ppermute(a, AXES, SIBLING)


def ahead(a, step):
    return lax.ppermute(a, AXES, [(r[i], r[(i + step) % 4]) for r in RINGS for i in range(4)])


def plane(a):
    return lax.all_to_all(a, AXES, 0, 0, axis_index_groups=PLANES, tiled=True)


def exchange(blocks):
    far = ahead(blocks[2], 2)
    return [blocks[0], ahead(blocks[3], 3), far, ahead(blocks[1], 1)]


def iota(shape, axis):
    return lax.broadcasted_iota(I32, shape, axis)


def pick(index, count):
    return jnp.where(index == iota((index.shape[0], count), 1), 1.0, 0.0).astype(BF16)


def coordinates():
    me = lax.axis_index("grp") * 64 + lax.axis_index("dev")
    z, x = (me >> 3) & 3, (me >> 1) & 3
    core = (me ^ x ^ z) & 1
    return core, me >> 2, jnp.where(core == 0, x, z), jnp.where(core == 0, z, x)


HBM = pl.BlockSpec(memory_space=pltpu.HBM)
VMEM = pl.BlockSpec(memory_space=pltpu.VMEM)


def attend_kernel(
    lens, query, cache, w_out, sent, out_other, q, kv, peak, total, acc, both, held, sems, kv_sems
):
    core, _, me_t, _ = coordinates()
    half = held.shape[1]
    away = pl.ds(pl.multiple_of((1 - core) * half, 128), half)
    take = pltpu.make_async_copy(w_out.at[:, away], held, sems.at[0])
    give = pltpu.make_async_copy(held, out_other, sems.at[1])
    ask = pltpu.make_async_copy(query, q, sems.at[2])

    def chunk(r, j):
        slots = pl.ds(pl.multiple_of(j * CHUNK, CHUNK), CHUNK)
        return pltpu.make_async_copy(cache.at[r, :, slots], kv.at[r, j], kv_sems.at[r, j])

    live = [(lens[r] + CHUNK - 1) // CHUNK for r in range(2)]
    ask.start()
    for r in range(2):

        @pl.loop(0, live[r])
        def _(j, r=r):
            chunk(r, j).start()

    take.start()
    ask.wait()
    for r in range(2):
        heads = lax.dot_general(
            pick(iota((128, 1), 0), 128), q[r], (((1,), (1,)), ((), ())), preferred_element_type=F32
        ).astype(BF16)
        peak[...] = jnp.full_like(peak, -1e30)
        total[...] = jnp.zeros_like(total)
        acc[...] = jnp.zeros_like(acc)

        @pl.loop(0, live[r])
        def _(j, r=r, heads=heads):
            chunk(r, j).wait()
            score = jnp.dot(heads, kv[r, j], preferred_element_type=F32)
            place = j * CHUNK + iota(score.shape, 1)
            score = jnp.where(place < lens[r], score * softmax_scale, -1e30)
            before = peak[...]
            now = jnp.maximum(before, jnp.max(score, axis=1, keepdims=True))
            fade = jnp.exp(before - now)
            weight = jnp.exp(score - now)
            peak[...] = now
            total[...] = total[...] * fade + jnp.sum(weight, axis=1, keepdims=True)
            acc[...] = acc[...] * fade + lax.dot_general(
                weight.astype(BF16),
                kv[r, j, :LATENT, :],
                (((1,), (1,)), ((), ())),
                preferred_element_type=F32,
            )

        both[r * 128 : r * 128 + 128, :] = (acc[...] / total[...]).astype(BF16)
        if r == 0:
            take.wait()
            give.start()

    i = iota((256, 1), 0)
    y, b, t = i >> 6, (i >> 4) & 3, (me_t + (i >> 2)) & 3
    z = jnp.where(core == 0, b, t)
    x = jnp.where(core == 0, t, b)
    head = device(y, z, x, ((i >> 1) & 1) ^ core)
    rows = jnp.dot(pick((i & 1) * 128 + head, 256), both[...], preferred_element_type=F32)
    sent[...] = rows.astype(BF16).reshape(sent.shape)
    give.wait()


def attend(lengths, queries, cache, w_out):
    _, size, heads = queries.shape
    half = w_out.shape[1] // 2
    chunks = cache.shape[2] // CHUNK
    return pl.pallas_call(
        attend_kernel,
        in_specs=[pl.BlockSpec(memory_space=pltpu.SMEM), HBM, HBM, HBM],
        out_specs=[VMEM, HBM],
        out_shape=[
            pltpu.VMEM((16, 16, LATENT), BF16),
            jax.ShapeDtypeStruct((VHEAD, half), BF16),
        ],
        scratch_shapes=[
            pltpu.VMEM((2, size, heads), BF16),
            pltpu.VMEM((2, chunks, size, CHUNK), BF16),
            pltpu.VMEM((heads, 1), F32),
            pltpu.VMEM((heads, 1), F32),
            pltpu.VMEM((heads, LATENT), F32),
            pltpu.VMEM((2 * heads, LATENT), BF16),
            pltpu.VMEM((VHEAD, half), BF16),
            pltpu.SemaphoreType.DMA((3,)),
            pltpu.SemaphoreType.DMA((2, chunks)),
        ],
        compiler_params=pltpu.CompilerParams(vmem_limit_bytes=56 * MIB),
        name="attend",
    )(lengths, queries, cache, w_out)


def load_kernel(places, *refs):
    arrays, (out, sems) = refs[: len(places)], refs[len(places) :]
    core = coordinates()[0]
    copies = []
    for n, (array, (axis, rows, columns)) in enumerate(zip(arrays, places)):
        if axis == 0:
            start = pl.multiple_of(core * out.shape[0], 128)
            array = array.at[pl.ds(start, out.shape[0]), :]
        if axis == 1:
            start = pl.multiple_of(core * out.shape[1], 128)
            array = array.at[:, pl.ds(start, out.shape[1])]
        copies.append(pltpu.make_async_copy(array, out.at[rows, columns], sems.at[n]))
    for copy in copies:
        copy.start()
    for copy in copies:
        copy.wait()


def load(arrays, places, shape, name, limit):
    size = 2 * shape[0] * shape[1]
    return pl.pallas_call(
        functools.partial(load_kernel, places),
        in_specs=[HBM] * len(arrays),
        out_specs=VMEM,
        out_shape=pltpu.VMEM(shape, BF16),
        scratch_shapes=[pltpu.SemaphoreType.DMA((len(arrays),))],
        compiler_params=pltpu.CompilerParams(vmem_limit_bytes=limit * MIB),
        cost_estimate=pl.CostEstimate(flops=0, bytes_accessed=2 * size, transcendentals=0),
        name=name,
    )(*arrays)


def pack_kernel(gate, up, down, after, gate_out, up_out, down_out, mark, *scratch):
    held, sems = scratch[:3], scratch[3]
    core = coordinates()[0]
    half = down_out.shape[1]
    away = pl.ds(pl.multiple_of((1 - core) * half, 128), half)
    sources = (gate.at[away, :], up.at[away, :], down.at[:, away])
    outs = (gate_out, up_out, down_out)
    takes = [pltpu.make_async_copy(a, b, sems.at[n]) for n, (a, b) in enumerate(zip(sources, held))]
    gives = [pltpu.make_async_copy(a, b, sems.at[3 + n]) for n, (a, b) in enumerate(zip(held, outs))]
    for take in takes:
        take.start()
    mark[...] = jnp.zeros_like(mark)
    for take, give in zip(takes, gives):
        take.wait()
        give.start()
    for give in gives:
        give.wait()


def pack(gate, up, down, after):
    half = down.shape[1] // 2
    shapes = [(half, 256), (half, 256), (256, half)]
    return pl.pallas_call(
        pack_kernel,
        in_specs=[HBM] * 3 + [pl.BlockSpec(memory_space=pl.ANY)],
        out_specs=[HBM] * 3 + [VMEM],
        out_shape=[jax.ShapeDtypeStruct(shape, BF16) for shape in shapes]
        + [pltpu.VMEM((8, 128), F32)],
        scratch_shapes=[pltpu.VMEM(shape, BF16) for shape in shapes]
        + [pltpu.SemaphoreType.DMA((6,))],
        compiler_params=pltpu.CompilerParams(vmem_limit_bytes=56 * MIB),
        cost_estimate=pl.CostEstimate(flops=0, bytes_accessed=12 * MIB, transcendentals=0),
        name="pack",
    )(gate, up, down, after)


def call(kernel, args, outs, name, flops, scratch=()):
    return pl.pallas_call(
        kernel,
        in_specs=[VMEM] * len(args),
        out_specs=[VMEM] * len(outs),
        out_shape=[jax.ShapeDtypeStruct(*out) for out in outs],
        scratch_shapes=list(scratch),
        compiler_params=pltpu.CompilerParams(vmem_limit_bytes=24 * MIB),
        cost_estimate=pl.CostEstimate(flops=flops, bytes_accessed=1 << 20, transcendentals=0),
        name=name,
    )(*args)


def turn_kernel(got, mark, o0, o1, o2, o3):
    rows = got[...].reshape(256, got.shape[2])
    i = iota((256, 1), 0)
    index = (i & 15) * 16 + (i >> 6) * 4 + ((i >> 4) & 3)
    rows = jnp.dot(pick(index, 256), rows, preferred_element_type=F32).astype(BF16)
    for d, out in enumerate((o0, o1, o2, o3)):
        out[...] = rows[d * 64 : d * 64 + 64]


def values_kernel(p0, p1, p2, p3, uv_own, uv_other, out):
    for head, uv in enumerate((uv_own, uv_other)):
        rows = jnp.concatenate(
            [p[head * 32 : head * 32 + 32, :] for p in (p0, p1, p2, p3)], axis=0
        )
        val = jnp.dot(rows, uv[...], preferred_element_type=F32)
        out[:, head * VHEAD : head * VHEAD + VHEAD] = val.astype(BF16)


PARTS = ((0, 64), (64, 96), (96, 128), (128, 160), (160, 192), (192, 224), (224, 256))


LATE = PARTS[:3] + PARTS[5:] + PARTS[3:5]


def put_parts(full, outs, columns, parts):
    for ref, (lo, hi) in zip(outs, parts):
        ref[:, columns] = full[lo:hi].astype(BF16)


def project_kernel(mine, theirs, w, *refs):
    outs, val = refs[:-1], refs[-1]
    _, _, me_t, me_p = coordinates()
    i = iota((128, 1), 0)
    t, b = ((i >> 5) + me_t) & 3, i & 3
    index = ((b - me_p) & 3) * 32 + (i & 0x1C) + t
    sib = jnp.dot(pick(index, 128), theirs[...], preferred_element_type=F32).astype(BF16)
    for d in range(4):
        for s, rows in enumerate((mine[...], sib)):
            at = d * 64 + s * 32
            rows = rows[d * 32 : d * 32 + 32]
            val[at : at + 32, s * VHEAD : s * VHEAD + VHEAD] = rows[:, :VHEAD]
            val[at : at + 32, (1 - s) * VHEAD : (2 - s) * VHEAD] = rows[:, VHEAD:]
    quarter = w.shape[1] // 4
    for q in range(4):
        columns = slice(q * quarter, (q + 1) * quarter)
        full = jnp.dot(val[...], w[:, columns], preferred_element_type=F32)
        put_parts(full, outs, columns, PARTS)


def product_outs(half):
    return [((hi - lo, half), BF16) for lo, hi in PARTS]


def gate_up_kernel(*refs):
    *refs, back, w, part, sent, squares, weight = refs
    count = part.shape[0]
    first = sent.shape[0] - count
    pieces = refs
    if first:
        before, *pieces = refs
        sent[:first, :] = before[...]
    sent = sent.at[pl.ds(first, count), :]
    expert = coordinates()[1]
    half = w.shape[0]
    quarter = half // 4
    sq = jnp.zeros((count, 1), F32)
    for q in range(4):
        columns = slice(q * quarter, (q + 1) * quarter)
        a = jnp.concatenate([p[:, columns] for p in pieces], axis=0)
        share = jnp.dot(a, w[columns, :], preferred_element_type=F32)
        if q == 0:
            part[...] = share
        else:
            part[...] += share
        plain = a.astype(F32) * back[:, columns]
        sq += jnp.sum(plain * plain, axis=1, keepdims=True)
    squares[...] = sq
    sent[:, :1024] = part[...].astype(BF16)
    hi = sq.astype(BF16).astype(F32)
    mid = (sq - hi).astype(BF16).astype(F32)
    lo = sq - hi - mid
    lane = iota((count, 128), 1)
    sent[:, 1024:] = jnp.where(
        lane == 0, hi, jnp.where(lane == 1, mid, jnp.where(lane == 2, lo, 0.0))
    ).astype(BF16)
    n = jnp.concatenate([p[:, half:] for p in pieces], axis=0).astype(F32)
    high = pltpu.roll(n, 128 - TOP, 1)
    low = pltpu.roll(n, 128 - 2 * TOP, 1)
    hit = (lane < TOP) & (n == expert.astype(F32))
    weight[...] = jnp.sum(jnp.where(hit, high + low, 0.0), axis=1, keepdims=True)


def gate_up(before, pieces, back, w):
    count = sum(p.shape[0] for p in pieces)
    rows = count + sum(b.shape[0] for b in before)
    return call(
        gate_up_kernel,
        (*before, *pieces, back, w),
        [((count, 1024), F32), ((rows, 1152), BF16), ((count, 1), F32), ((count, 1), F32)],
        "gate_up",
        count << 23,
    )


def late(d):
    return d ^ (d >> 1)


def down_kernel(p0, q0, w0, p1, q1, w1, got, w, *refs):
    outs, hidden = refs[:-1], refs[-1]
    _, _, me_t, me_p = coordinates()
    i = iota((256, 1), 0)
    d, s, rest = late(i >> 6), (i >> 5) & 1, i & 0x1C
    t, b = (d + me_t) & 3, i & 3
    index = late((b - me_p) & 3) * 64 + (1 - s) * 32 + rest + t
    theirs = jnp.dot(pick(index, 256), got[...], preferred_element_type=F32)
    at = 0
    for part, squares in ((p0, q0), (p1, q1)):
        rows = slice(at, at + part.shape[0])
        at += part.shape[0]
        tail = theirs[rows, 1024:]
        lane = iota(tail.shape, 1)
        sq = squares[...] + jnp.sum(jnp.where(lane < 3, tail, 0.0), axis=1, keepdims=True)
        scale = lax.rsqrt(sq / 7168.0 + 1e-06)
        for block in range(2):
            left, right = block * 512, 512 - block * 512
            gate = (part[:, left : left + 256] + theirs[rows, right : right + 256]) * scale
            left, right = left + 256, right + 256
            up = (part[:, left : left + 256] + theirs[rows, right : right + 256]) * scale
            hidden[rows, block * 256 : block * 256 + 256] = (
                gate / (1.0 + jnp.exp(-gate)) * up
            ).astype(BF16)
    weight = jnp.concatenate([w0[...], w1[...]], axis=0)
    quarter = w.shape[1] // 4
    for q in range(4):
        columns = slice(q * quarter, (q + 1) * quarter)
        full = jnp.dot(hidden[...], w[:, columns], preferred_element_type=F32)
        put_parts(full * weight, outs, columns, LATE)


def add(a, b):
    return (a.astype(F32) + b.astype(F32)).astype(BF16)


def reduce_rows(b0, b1t, b1b, b2t, b2b, b3t, b3b):
    far_left, far_right = ahead(b2t, 1), ahead(b2b, -1)
    left_b, right_t = ahead(b1b, 1), ahead(b3t, -1)
    left_t, right_b = ahead(add(b1t, far_left), 1), ahead(add(b3b, far_right), -1)
    left = jnp.concatenate([left_t, left_b])
    right = jnp.concatenate([right_t, right_b])
    mine = (b0.astype(F32) + left.astype(F32) + right.astype(F32)).astype(BF16)
    mine = mine.reshape(4, 16, mine.shape[1]).swapaxes(0, 1)
    return jnp.sum(plane(mine).astype(F32), axis=0)


def gather_rows(a):
    a0 = plane(jnp.broadcast_to(a, (16, *a.shape)))
    a0 = a0.swapaxes(0, 1).reshape(64, a.shape[1])
    top, bottom = a0[:32], a0[32:]
    left_t, right_b = ahead(top, 1), ahead(bottom, -1)
    left_b, right_t = ahead(bottom, 1), ahead(top, -1)
    return (a0, right_t, right_b, left_t, left_b), (ahead(left_t, 1), ahead(right_b, -1))


def shards(queries, cache, lengths, w_uv, w_out, residual, gain, ids, gates, w_gate, w_up, w_down):
    me = lax.axis_index(AXES)
    core = (me ^ (me >> 1) ^ (me >> 3)) & 1
    half = residual.shape[1] // 2

    def own(w, axis):
        return lax.dynamic_slice_in_dim(w, core * half, half, axis)

    def away(w, axis):
        return lax.dynamic_slice_in_dim(w, (1 - core) * half, half, axis)

    sent, out_other = attend(lengths, queries.swapaxes(1, 2), cache.swapaxes(1, 2), w_out)
    uv_other = swap(w_uv[0])
    *packed, mark = pack(w_gate[0], w_up[0], w_down[0], out_other)
    blocks = pl.pallas_call(
        turn_kernel,
        in_specs=[VMEM, VMEM],
        out_specs=[VMEM] * 4,
        out_shape=[jax.ShapeDtypeStruct((64, LATENT), BF16)] * 4,
        compiler_params=pltpu.CompilerParams(vmem_limit_bytes=16 * MIB),
        name="turn",
    )(plane(sent), mark)
    blocks = exchange(blocks)
    out_other = swap(out_other)
    every = slice(None)
    w_out = load(
        (w_out, out_other),
        ((1, slice(0, VHEAD), every), (None, slice(VHEAD, 2 * VHEAD), every)),
        (2 * VHEAD, half),
        "load_out",
        8,
    )
    (mine,) = call(
        values_kernel,
        (*blocks, w_uv[0], uv_other),
        [((128, 2 * VHEAD), BF16)],
        "values",
        1 << 25,
    )
    gate_other, up_other, down_other = (swap(a) for a in packed)

    gates_hi = gates.astype(BF16)
    gates_lo = (gates - gates_hi.astype(F32)).astype(BF16)
    names = jnp.concatenate(
        [ids.astype(BF16), gates_hi, gates_lo, jnp.zeros((2, 128 - 3 * TOP), BF16)], axis=1
    )
    rows = jnp.concatenate(
        [
            jnp.concatenate([own(residual, 1), names], axis=1),
            swap(jnp.concatenate([away(residual, 1), names], axis=1)),
        ]
    )
    res, names = rows[:, :half].astype(F32), rows[:, half:]

    pieces = call(
        project_kernel,
        (mine, swap(mine), w_out),
        product_outs(half),
        "project",
        1 << 29,
        [pltpu.VMEM((256, 2 * VHEAD), BF16)],
    )
    mixed = res + reduce_rows(*pieces)

    scaled = (mixed * own(gain, 0)).astype(BF16)
    w_gu = load(
        (w_gate[0], w_up[0], gate_other, up_other),
        tuple((0 if n < 2 else None, every, slice(256 * n, 256 * n + 256)) for n in range(4)),
        (half, 1024),
        "load_gate_up",
        42,
    )
    near, far = gather_rows(jnp.concatenate([scaled, names], axis=1))
    back = (1.0 / own(gain, 0)).reshape(1, half)
    p0, sent, q0, w0 = gate_up((), near, back, w_gu)
    p1, sent, q1, w1 = gate_up((sent,), far, back, w_gu)
    w_down = load(
        (w_down[0], down_other),
        ((1, slice(0, 256), every), (None, slice(256, 512), every)),
        (512, half),
        "load_down",
        46,
    )
    pieces = call(
        down_kernel,
        (p0, q0, w0, p1, q1, w1, swap(sent), w_down),
        product_outs(half),
        "down",
        1 << 30,
        [pltpu.VMEM((256, 512), BF16)],
    )
    result = (mixed + reduce_rows(*pieces)).astype(BF16)

    mine, other = result[:2], swap(result[2:])
    return jnp.where(
        core == 0, jnp.concatenate([mine, other], 1), jnp.concatenate([other, mine], 1)
    )


def solution(mesh):
    in_specs = (
        P(("grp", "dev"), None, None),
        P(("grp", "dev"), None, None),
        P(("grp", "dev")),
        P(("grp", "dev"), None, None),
        P(("grp", "dev"), None),
        P(("grp", "dev"), None),
        P(),
        P(("grp", "dev"), None),
        P(("grp", "dev"), None),
        P(("grp", "dev"), None, None),
        P(("grp", "dev"), None, None),
        P(("grp", "dev"), None, None),
    )
    out_specs = P(("grp", "dev"), None)
    return jax.shard_map(shards, mesh=mesh, in_specs=in_specs, out_specs=out_specs, check_vma=False)
```

```python
import functools

import jax
import jax.numpy as jnp
from jax import lax
from jax.experimental import pallas as pl
from jax.experimental.pallas import tpu as pltpu
from jax.sharding import PartitionSpec as P

LATENT = 512
VHEAD = 128
TOP = 8
AXES = ("grp", "dev")
F32 = jnp.float32
BF16 = jnp.bfloat16
I32 = jnp.int32
MIB = 1 << 20
CHUNK = 1024

softmax_scale = 192.0 ** (-0.5)


def device(y, z, x, c):
    return ((y * 4 + z) * 4 + x) * 2 + (c ^ ((x + z) & 1))


RINGS = [[device(y, z, x, 0) for x in range(4)] for y in range(4) for z in range(4)] + [
    [device(y, z, x, 1) for z in range(4)] for y in range(4) for x in range(4)
]
PLANES = [[device(y, z, x, 0) for y in range(4) for z in range(4)] for x in range(4)] + [
    [device(y, z, x, 1) for y in range(4) for x in range(4)] for z in range(4)
]
SIBLING = [(i, i ^ 1) for i in range(128)]


def swap(a):
    return lax.ppermute(a, AXES, SIBLING)


def ahead(a, step):
    return lax.ppermute(a, AXES, [(r[i], r[(i + step) % 4]) for r in RINGS for i in range(4)])


def plane(a):
    return lax.all_to_all(a, AXES, 0, 0, axis_index_groups=PLANES, tiled=True)


def exchange(blocks):
    far = ahead(blocks[2], 2)
    return [blocks[0], ahead(blocks[3], 3), far, ahead(blocks[1], 1)]


def iota(shape, axis):
    return lax.broadcasted_iota(I32, shape, axis)


def pick(index, count):
    return jnp.where(index == iota((index.shape[0], count), 1), 1.0, 0.0).astype(BF16)


def coordinates():
    me = lax.axis_index("grp") * 64 + lax.axis_index("dev")
    z, x = (me >> 3) & 3, (me >> 1) & 3
    core = (me ^ x ^ z) & 1
    return core, me >> 2, jnp.where(core == 0, x, z), jnp.where(core == 0, z, x)


HBM = pl.BlockSpec(memory_space=pltpu.HBM)
VMEM = pl.BlockSpec(memory_space=pltpu.VMEM)


def attend_kernel(
    lens, query, cache, w_out, sent, out_other, q, kv, peak, total, acc, both, held, sems, kv_sems
):
    core, _, me_t, _ = coordinates()
    half = held.shape[1]
    away = pl.ds(pl.multiple_of((1 - core) * half, 128), half)
    take = pltpu.make_async_copy(w_out.at[:, away], held, sems.at[0])
    give = pltpu.make_async_copy(held, out_other, sems.at[1])
    ask = pltpu.make_async_copy(query, q, sems.at[2])

    def chunk(r, j):
        slots = pl.ds(pl.multiple_of(j * CHUNK, CHUNK), CHUNK)
        return pltpu.make_async_copy(cache.at[r, :, slots], kv.at[r, j], kv_sems.at[r, j])

    live = [(lens[r] + CHUNK - 1) // CHUNK for r in range(2)]
    ask.start()
    for r in range(2):

        @pl.loop(0, live[r])
        def _(j, r=r):
            chunk(r, j).start()

    take.start()
    ask.wait()
    for r in range(2):
        heads = lax.dot_general(
            pick(iota((128, 1), 0), 128), q[r], (((1,), (1,)), ((), ())), preferred_element_type=F32
        ).astype(BF16)
        peak[...] = jnp.full_like(peak, -1e30)
        total[...] = jnp.zeros_like(total)
        acc[...] = jnp.zeros_like(acc)

        @pl.loop(0, live[r])
        def _(j, r=r, heads=heads):
            chunk(r, j).wait()
            score = jnp.dot(heads, kv[r, j], preferred_element_type=F32)
            place = j * CHUNK + iota(score.shape, 1)
            score = jnp.where(place < lens[r], score * softmax_scale, -1e30)
            before = peak[...]
            now = jnp.maximum(before, jnp.max(score, axis=1, keepdims=True))
            fade = jnp.exp(before - now)
            weight = jnp.exp(score - now)
            peak[...] = now
            total[...] = total[...] * fade + jnp.sum(weight, axis=1, keepdims=True)
            acc[...] = acc[...] * fade + lax.dot_general(
                weight.astype(BF16),
                kv[r, j, :LATENT, :],
                (((1,), (1,)), ((), ())),
                preferred_element_type=F32,
            )

        both[r * 128 : r * 128 + 128, :] = (acc[...] / total[...]).astype(BF16)
        if r == 0:
            take.wait()
            give.start()

    i = iota((256, 1), 0)
    y, b, t = i >> 6, (i >> 4) & 3, (me_t + (i >> 2)) & 3
    z = jnp.where(core == 0, b, t)
    x = jnp.where(core == 0, t, b)
    head = device(y, z, x, ((i >> 1) & 1) ^ core)
    rows = jnp.dot(pick((i & 1) * 128 + head, 256), both[...], preferred_element_type=F32)
    sent[...] = rows.astype(BF16).reshape(sent.shape)
    give.wait()


def attend(lengths, queries, cache, w_out):
    _, size, heads = queries.shape
    half = w_out.shape[1] // 2
    chunks = cache.shape[2] // CHUNK
    return pl.pallas_call(
        attend_kernel,
        in_specs=[pl.BlockSpec(memory_space=pltpu.SMEM), HBM, HBM, HBM],
        out_specs=[VMEM, HBM],
        out_shape=[
            pltpu.VMEM((16, 16, LATENT), BF16),
            jax.ShapeDtypeStruct((VHEAD, half), BF16),
        ],
        scratch_shapes=[
            pltpu.VMEM((2, size, heads), BF16),
            pltpu.VMEM((2, chunks, size, CHUNK), BF16),
            pltpu.VMEM((heads, 1), F32),
            pltpu.VMEM((heads, 1), F32),
            pltpu.VMEM((heads, LATENT), F32),
            pltpu.VMEM((2 * heads, LATENT), BF16),
            pltpu.VMEM((VHEAD, half), BF16),
            pltpu.SemaphoreType.DMA((3,)),
            pltpu.SemaphoreType.DMA((2, chunks)),
        ],
        compiler_params=pltpu.CompilerParams(vmem_limit_bytes=56 * MIB),
        name="attend",
    )(lengths, queries, cache, w_out)


def load_kernel(places, *refs):
    *arrays, out, sems = refs
    core = coordinates()[0]
    copies = []
    for n, (which, part, rows, columns) in enumerate(places):
        array = arrays[which]
        if part == 0:
            start = pl.multiple_of(core * out.shape[0], 128)
            array = array.at[pl.ds(start, out.shape[0]), :]
        elif part == 1:
            start = pl.multiple_of(core * out.shape[1], 128)
            array = array.at[:, pl.ds(start, out.shape[1])]
        else:
            array = array.at[part, :]
        copies.append(pltpu.make_async_copy(array, out.at[rows, columns], sems.at[n]))
    for copy in copies:
        copy.start()
    for copy in copies:
        copy.wait()


def load(arrays, places, shape, name, limit):
    size = 2 * shape[0] * shape[1]
    return pl.pallas_call(
        functools.partial(load_kernel, places),
        in_specs=[HBM] * len(arrays),
        out_specs=VMEM,
        out_shape=pltpu.VMEM(shape, BF16),
        scratch_shapes=[pltpu.SemaphoreType.DMA((len(places),))],
        compiler_params=pltpu.CompilerParams(vmem_limit_bytes=limit * MIB),
        cost_estimate=pl.CostEstimate(flops=0, bytes_accessed=2 * size, transcendentals=0),
        name=name,
    )(*arrays)


def pack_kernel(gate, up, down, after, out, mark, held, sems):
    core = coordinates()[0]
    half = gate.shape[0] // 2
    start = (1 - core) * half
    away = pl.ds(pl.multiple_of(start, 128), half)
    takes = [
        pltpu.make_async_copy(gate.at[away, :], held.at[pl.ds(0, half), :], sems.at[0]),
        pltpu.make_async_copy(up.at[away, :], held.at[pl.ds(half, half), :], sems.at[1]),
    ]
    for n in range(half // 256):
        columns = pl.ds(pl.multiple_of(start + n * 256, 128), 256)
        rows = pl.ds(2 * half + n * 256, 256)
        takes.append(pltpu.make_async_copy(down.at[:, columns], held.at[rows, :], sems.at[2 + n]))
    gives = []
    for n in range(3):
        rows = pl.ds(n * half, half)
        gives.append(
            pltpu.make_async_copy(held.at[rows, :], out.at[rows, :], sems.at[len(takes) + n])
        )
    for take in takes:
        take.start()
    mark[...] = jnp.zeros_like(mark)
    for n, give in enumerate(gives):
        for take in takes[n : n + 1] if n < 2 else takes[2:]:
            take.wait()
        give.start()
    for give in gives:
        give.wait()


def pack(gate, up, down, after):
    half = gate.shape[0] // 2
    return pl.pallas_call(
        pack_kernel,
        in_specs=[HBM] * 3 + [pl.BlockSpec(memory_space=pl.ANY)],
        out_specs=[HBM, VMEM],
        out_shape=[jax.ShapeDtypeStruct((3 * half, 256), BF16), pltpu.VMEM((8, 128), F32)],
        scratch_shapes=[
            pltpu.VMEM((3 * half, 256), BF16),
            pltpu.SemaphoreType.DMA((5 + half // 256,)),
        ],
        compiler_params=pltpu.CompilerParams(vmem_limit_bytes=56 * MIB),
        cost_estimate=pl.CostEstimate(flops=0, bytes_accessed=12 * MIB, transcendentals=0),
        name="pack",
    )(gate, up, down, after)


def call(kernel, args, outs, name, flops, scratch=()):
    return pl.pallas_call(
        kernel,
        in_specs=[VMEM] * len(args),
        out_specs=[VMEM] * len(outs),
        out_shape=[jax.ShapeDtypeStruct(*out) for out in outs],
        scratch_shapes=list(scratch),
        compiler_params=pltpu.CompilerParams(vmem_limit_bytes=24 * MIB),
        cost_estimate=pl.CostEstimate(flops=flops, bytes_accessed=1 << 20, transcendentals=0),
        name=name,
    )(*args)


def turn_kernel(got, mark, o0, o1, o2, o3):
    rows = got[...].reshape(256, got.shape[2])
    i = iota((256, 1), 0)
    index = (i & 15) * 16 + (i >> 6) * 4 + ((i >> 4) & 3)
    rows = jnp.dot(pick(index, 256), rows, preferred_element_type=F32).astype(BF16)
    for d, out in enumerate((o0, o1, o2, o3)):
        out[...] = rows[d * 64 : d * 64 + 64]


def values_kernel(p0, p1, p2, p3, uv_own, uv_other, out):
    for head, uv in enumerate((uv_own, uv_other)):
        rows = jnp.concatenate(
            [p[head * 32 : head * 32 + 32, :] for p in (p0, p1, p2, p3)], axis=0
        )
        val = jnp.dot(rows, uv[...], preferred_element_type=F32)
        out[:, head * VHEAD : head * VHEAD + VHEAD] = val.astype(BF16)


PARTS = ((0, 64), (64, 96), (96, 128), (128, 160), (160, 192), (192, 224), (224, 256))


LATE = PARTS[:3] + PARTS[5:] + PARTS[3:5]


def put_parts(full, outs, columns, parts):
    for ref, (lo, hi) in zip(outs, parts):
        ref[:, columns] = full[lo:hi].astype(BF16)


def project_kernel(mine, theirs, w, *refs):
    outs, val = refs[:-1], refs[-1]
    _, _, me_t, me_p = coordinates()
    i = iota((128, 1), 0)
    t, b = ((i >> 5) + me_t) & 3, i & 3
    index = ((b - me_p) & 3) * 32 + (i & 0x1C) + t
    sib = jnp.dot(pick(index, 128), theirs[...], preferred_element_type=F32).astype(BF16)
    for d in range(4):
        for s, rows in enumerate((mine[...], sib)):
            at = d * 64 + s * 32
            rows = rows[d * 32 : d * 32 + 32]
            val[at : at + 32, s * VHEAD : s * VHEAD + VHEAD] = rows[:, :VHEAD]
            val[at : at + 32, (1 - s) * VHEAD : (2 - s) * VHEAD] = rows[:, VHEAD:]
    quarter = w.shape[1] // 4
    for q in range(4):
        columns = slice(q * quarter, (q + 1) * quarter)
        full = jnp.dot(val[...], w[:, columns], preferred_element_type=F32)
        put_parts(full, outs, columns, PARTS)


def product_outs(half):
    return [((hi - lo, half), BF16) for lo, hi in PARTS]


def gate_up_kernel(*refs):
    *refs, back, w, part, sent, squares, weight = refs
    count = part.shape[0]
    first = sent.shape[0] - count
    pieces = refs
    if first:
        before, *pieces = refs
        sent[:first, :] = before[...]
    sent = sent.at[pl.ds(first, count), :]
    expert = coordinates()[1]
    half = w.shape[0]
    quarter = half // 4
    sq = jnp.zeros((count, 1), F32)
    for q in range(4):
        columns = slice(q * quarter, (q + 1) * quarter)
        a = jnp.concatenate([p[:, columns] for p in pieces], axis=0)
        share = jnp.dot(a, w[columns, :], preferred_element_type=F32)
        if q == 0:
            part[...] = share
        else:
            part[...] += share
        plain = a.astype(F32) * back[:, columns]
        sq += jnp.sum(plain * plain, axis=1, keepdims=True)
    squares[...] = sq
    sent[:, :1024] = part[...].astype(BF16)
    hi = sq.astype(BF16).astype(F32)
    mid = (sq - hi).astype(BF16).astype(F32)
    lo = sq - hi - mid
    lane = iota((count, 128), 1)
    sent[:, 1024:] = jnp.where(
        lane == 0, hi, jnp.where(lane == 1, mid, jnp.where(lane == 2, lo, 0.0))
    ).astype(BF16)
    n = jnp.concatenate([p[:, half:] for p in pieces], axis=0).astype(F32)
    high = pltpu.roll(n, 128 - TOP, 1)
    low = pltpu.roll(n, 128 - 2 * TOP, 1)
    hit = (lane < TOP) & (n == expert.astype(F32))
    weight[...] = jnp.sum(jnp.where(hit, high + low, 0.0), axis=1, keepdims=True)


def gate_up(before, pieces, back, w):
    count = sum(p.shape[0] for p in pieces)
    rows = count + sum(b.shape[0] for b in before)
    return call(
        gate_up_kernel,
        (*before, *pieces, back, w),
        [((count, 1024), F32), ((rows, 1152), BF16), ((count, 1), F32), ((count, 1), F32)],
        "gate_up",
        count << 23,
    )


def late(d):
    return d ^ (d >> 1)


def down_kernel(p0, q0, w0, p1, q1, w1, got, w, *refs):
    outs, hidden = refs[:-1], refs[-1]
    _, _, me_t, me_p = coordinates()
    i = iota((256, 1), 0)
    d, s, rest = late(i >> 6), (i >> 5) & 1, i & 0x1C
    t, b = (d + me_t) & 3, i & 3
    index = late((b - me_p) & 3) * 64 + (1 - s) * 32 + rest + t
    theirs = jnp.dot(pick(index, 256), got[...], preferred_element_type=F32)
    at = 0
    for part, squares in ((p0, q0), (p1, q1)):
        rows = slice(at, at + part.shape[0])
        at += part.shape[0]
        tail = theirs[rows, 1024:]
        lane = iota(tail.shape, 1)
        sq = squares[...] + jnp.sum(jnp.where(lane < 3, tail, 0.0), axis=1, keepdims=True)
        scale = lax.rsqrt(sq / 7168.0 + 1e-06)
        for block in range(2):
            left, right = block * 512, 512 - block * 512
            gate = (part[:, left : left + 256] + theirs[rows, right : right + 256]) * scale
            left, right = left + 256, right + 256
            up = (part[:, left : left + 256] + theirs[rows, right : right + 256]) * scale
            hidden[rows, block * 256 : block * 256 + 256] = (
                gate / (1.0 + jnp.exp(-gate)) * up
            ).astype(BF16)
    weight = jnp.concatenate([w0[...], w1[...]], axis=0)
    quarter = w.shape[1] // 4
    for q in range(4):
        columns = slice(q * quarter, (q + 1) * quarter)
        full = jnp.dot(hidden[...], w[:, columns], preferred_element_type=F32)
        put_parts(full * weight, outs, columns, LATE)


def add(a, b):
    return (a.astype(F32) + b.astype(F32)).astype(BF16)


def reduce_rows(b0, b1t, b1b, b2t, b2b, b3t, b3b):
    far_left, far_right = ahead(b2t, 1), ahead(b2b, -1)
    left_b, right_t = ahead(b1b, 1), ahead(b3t, -1)
    left_t, right_b = ahead(add(b1t, far_left), 1), ahead(add(b3b, far_right), -1)
    left = jnp.concatenate([left_t, left_b])
    right = jnp.concatenate([right_t, right_b])
    mine = (b0.astype(F32) + left.astype(F32) + right.astype(F32)).astype(BF16)
    mine = mine.reshape(4, 16, mine.shape[1]).swapaxes(0, 1)
    return jnp.sum(plane(mine).astype(F32), axis=0)


def gather_rows(a):
    a0 = plane(jnp.broadcast_to(a, (16, *a.shape)))
    a0 = a0.swapaxes(0, 1).reshape(64, a.shape[1])
    top, bottom = a0[:32], a0[32:]
    left_t, right_b = ahead(top, 1), ahead(bottom, -1)
    left_b, right_t = ahead(bottom, 1), ahead(top, -1)
    return (a0, right_t, right_b, left_t, left_b), (ahead(left_t, 1), ahead(right_b, -1))


def shards(queries, cache, lengths, w_uv, w_out, residual, gain, ids, gates, w_gate, w_up, w_down):
    me = lax.axis_index(AXES)
    core = (me ^ (me >> 1) ^ (me >> 3)) & 1
    half = residual.shape[1] // 2

    def own(w, axis):
        return lax.dynamic_slice_in_dim(w, core * half, half, axis)

    def away(w, axis):
        return lax.dynamic_slice_in_dim(w, (1 - core) * half, half, axis)

    sent, out_other = attend(lengths, queries.swapaxes(1, 2), cache.swapaxes(1, 2), w_out)
    uv_other = swap(w_uv[0])
    packed, mark = pack(w_gate[0], w_up[0], w_down[0], out_other)
    blocks = pl.pallas_call(
        turn_kernel,
        in_specs=[VMEM, VMEM],
        out_specs=[VMEM] * 4,
        out_shape=[jax.ShapeDtypeStruct((64, LATENT), BF16)] * 4,
        compiler_params=pltpu.CompilerParams(vmem_limit_bytes=16 * MIB),
        name="turn",
    )(plane(sent), mark)
    blocks = exchange(blocks)
    out_other = swap(out_other)
    every = slice(None)
    w_out = load(
        (w_out, out_other),
        ((0, 1, slice(0, VHEAD), every), (1, every, slice(VHEAD, 2 * VHEAD), every)),
        (2 * VHEAD, half),
        "load_out",
        8,
    )
    (mine,) = call(
        values_kernel,
        (*blocks, w_uv[0], uv_other),
        [((128, 2 * VHEAD), BF16)],
        "values",
        1 << 25,
    )
    packed = swap(packed)

    gates_hi = gates.astype(BF16)
    gates_lo = (gates - gates_hi.astype(F32)).astype(BF16)
    names = jnp.concatenate(
        [ids.astype(BF16), gates_hi, gates_lo, jnp.zeros((2, 128 - 3 * TOP), BF16)], axis=1
    )
    rows = jnp.concatenate(
        [
            jnp.concatenate([own(residual, 1), names], axis=1),
            swap(jnp.concatenate([away(residual, 1), names], axis=1)),
        ]
    )
    res, names = rows[:, :half].astype(F32), rows[:, half:]

    pieces = call(
        project_kernel,
        (mine, swap(mine), w_out),
        product_outs(half),
        "project",
        1 << 29,
        [pltpu.VMEM((256, 2 * VHEAD), BF16)],
    )
    mixed = res + reduce_rows(*pieces)

    scaled = (mixed * own(gain, 0)).astype(BF16)
    w_gu = load(
        (w_gate[0], w_up[0], packed),
        (
            (0, 0, every, slice(0, 256)),
            (1, 0, every, slice(256, 512)),
            (2, slice(0, half), every, slice(512, 768)),
            (2, slice(half, 2 * half), every, slice(768, 1024)),
        ),
        (half, 1024),
        "load_gate_up",
        42,
    )
    near, far = gather_rows(jnp.concatenate([scaled, names], axis=1))
    back = (1.0 / own(gain, 0)).reshape(1, half)
    p0, sent, q0, w0 = gate_up((), near, back, w_gu)
    p1, sent, q1, w1 = gate_up((sent,), far, back, w_gu)
    w_down = load(
        (w_down[0], packed),
        (
            (0, 1, slice(0, 256), every),
            *(
                (1, slice(2 * half + n, 2 * half + n + 256), slice(256, 512), slice(n, n + 256))
                for n in range(0, half, 256)
            ),
        ),
        (512, half),
        "load_down",
        46,
    )
    pieces = call(
        down_kernel,
        (p0, q0, w0, p1, q1, w1, swap(sent), w_down),
        product_outs(half),
        "down",
        1 << 30,
        [pltpu.VMEM((256, 512), BF16)],
    )
    result = (mixed + reduce_rows(*pieces)).astype(BF16)

    mine, other = result[:2], swap(result[2:])
    return jnp.where(
        core == 0, jnp.concatenate([mine, other], 1), jnp.concatenate([other, mine], 1)
    )


def solution(mesh):
    in_specs = (
        P(("grp", "dev"), None, None),
        P(("grp", "dev"), None, None),
        P(("grp", "dev")),
        P(("grp", "dev"), None, None),
        P(("grp", "dev"), None),
        P(("grp", "dev"), None),
        P(),
        P(("grp", "dev"), None),
        P(("grp", "dev"), None),
        P(("grp", "dev"), None, None),
        P(("grp", "dev"), None, None),
        P(("grp", "dev"), None, None),
    )
    out_specs = P(("grp", "dev"), None)
    return jax.shard_map(shards, mesh=mesh, in_specs=in_specs, out_specs=out_specs, check_vma=False)
```

```python
import functools

import jax
import jax.numpy as jnp
from jax import lax
from jax.experimental import pallas as pl
from jax.experimental.pallas import tpu as pltpu
from jax.sharding import PartitionSpec as P

LATENT = 512
VHEAD = 128
TOP = 8
AXES = ("grp", "dev")
F32 = jnp.float32
BF16 = jnp.bfloat16
I32 = jnp.int32
MIB = 1 << 20
CHUNK = 1024

softmax_scale = 192.0 ** (-0.5)


def device(y, z, x, c):
    return ((y * 4 + z) * 4 + x) * 2 + (c ^ ((x + z) & 1))


RINGS = [[device(y, z, x, 0) for x in range(4)] for y in range(4) for z in range(4)] + [
    [device(y, z, x, 1) for z in range(4)] for y in range(4) for x in range(4)
]
PLANES = [[device(y, z, x, 0) for y in range(4) for z in range(4)] for x in range(4)] + [
    [device(y, z, x, 1) for y in range(4) for x in range(4)] for z in range(4)
]
SIBLING = [(i, i ^ 1) for i in range(128)]


def swap(a):
    return lax.ppermute(a, AXES, SIBLING)


def ahead(a, step):
    return lax.ppermute(a, AXES, [(r[i], r[(i + step) % 4]) for r in RINGS for i in range(4)])


def plane(a):
    return lax.all_to_all(a, AXES, 0, 0, axis_index_groups=PLANES, tiled=True)


def exchange(blocks):
    far = ahead(blocks[2], 2)
    return [blocks[0], ahead(blocks[3], 3), far, ahead(blocks[1], 1)]


def iota(shape, axis):
    return lax.broadcasted_iota(I32, shape, axis)


def pick(index, count):
    return jnp.where(index == iota((index.shape[0], count), 1), 1.0, 0.0).astype(BF16)


def coordinates():
    me = lax.axis_index("grp") * 64 + lax.axis_index("dev")
    z, x = (me >> 3) & 3, (me >> 1) & 3
    core = (me ^ x ^ z) & 1
    return core, me >> 2, jnp.where(core == 0, x, z), jnp.where(core == 0, z, x)


HBM = pl.BlockSpec(memory_space=pltpu.HBM)
VMEM = pl.BlockSpec(memory_space=pltpu.VMEM)


def attend_kernel(
    lens, query, cache, w_out, sent, out_other, q, kv, peak, total, acc, both, held, sems, kv_sems
):
    core, _, me_t, _ = coordinates()
    half = held.shape[1]
    away = pl.ds(pl.multiple_of((1 - core) * half, 128), half)
    take = pltpu.make_async_copy(w_out.at[:, away], held, sems.at[0])
    give = pltpu.make_async_copy(held, out_other, sems.at[1])
    ask = pltpu.make_async_copy(query, q, sems.at[2])

    def chunk(r, j):
        slots = pl.ds(pl.multiple_of(j * CHUNK, CHUNK), CHUNK)
        return pltpu.make_async_copy(cache.at[r, :, slots], kv.at[r, j], kv_sems.at[r, j])

    live = [(lens[r] + CHUNK - 1) // CHUNK for r in range(2)]
    ask.start()
    for r in range(2):

        @pl.loop(0, live[r])
        def _(j, r=r):
            chunk(r, j).start()

    take.start()
    ask.wait()
    for r in range(2):
        heads = lax.dot_general(
            pick(iota((128, 1), 0), 128), q[r], (((1,), (1,)), ((), ())), preferred_element_type=F32
        ).astype(BF16)
        peak[...] = jnp.full_like(peak, -1e30)
        total[...] = jnp.zeros_like(total)
        acc[...] = jnp.zeros_like(acc)

        @pl.loop(0, live[r])
        def _(j, r=r, heads=heads):
            chunk(r, j).wait()
            score = jnp.dot(heads, kv[r, j], preferred_element_type=F32)
            place = j * CHUNK + iota(score.shape, 1)
            score = jnp.where(place < lens[r], score * softmax_scale, -1e30)
            before = peak[...]
            now = jnp.maximum(before, jnp.max(score, axis=1, keepdims=True))
            fade = jnp.exp(before - now)
            weight = jnp.exp(score - now)
            peak[...] = now
            total[...] = total[...] * fade + jnp.sum(weight, axis=1, keepdims=True)
            acc[...] = acc[...] * fade + lax.dot_general(
                weight.astype(BF16),
                kv[r, j, :LATENT, :],
                (((1,), (1,)), ((), ())),
                preferred_element_type=F32,
            )

        both[r * 128 : r * 128 + 128, :] = (acc[...] / total[...]).astype(BF16)
        if r == 0:
            take.wait()
            give.start()

    i = iota((256, 1), 0)
    y, b, t = i >> 6, (i >> 4) & 3, (me_t + (i >> 2)) & 3
    z = jnp.where(core == 0, b, t)
    x = jnp.where(core == 0, t, b)
    head = device(y, z, x, ((i >> 1) & 1) ^ core)
    rows = jnp.dot(pick((i & 1) * 128 + head, 256), both[...], preferred_element_type=F32)
    sent[...] = rows.astype(BF16).reshape(sent.shape)
    give.wait()


def attend(lengths, queries, cache, w_out):
    _, size, heads = queries.shape
    half = w_out.shape[1] // 2
    chunks = cache.shape[2] // CHUNK
    return pl.pallas_call(
        attend_kernel,
        in_specs=[pl.BlockSpec(memory_space=pltpu.SMEM), HBM, HBM, HBM],
        out_specs=[VMEM, HBM],
        out_shape=[
            pltpu.VMEM((16, 16, LATENT), BF16),
            jax.ShapeDtypeStruct((VHEAD, half), BF16),
        ],
        scratch_shapes=[
            pltpu.VMEM((2, size, heads), BF16),
            pltpu.VMEM((2, chunks, size, CHUNK), BF16),
            pltpu.VMEM((heads, 1), F32),
            pltpu.VMEM((heads, 1), F32),
            pltpu.VMEM((heads, LATENT), F32),
            pltpu.VMEM((2 * heads, LATENT), BF16),
            pltpu.VMEM((VHEAD, half), BF16),
            pltpu.SemaphoreType.DMA((3,)),
            pltpu.SemaphoreType.DMA((2, chunks)),
        ],
        compiler_params=pltpu.CompilerParams(vmem_limit_bytes=56 * MIB),
        name="attend",
    )(lengths, queries, cache, w_out)


def load_kernel(places, *refs):
    *arrays, out, sems = refs
    core = coordinates()[0]
    copies = []
    for n, (which, part, rows, columns) in enumerate(places):
        array = arrays[which]
        if part == 0:
            start = pl.multiple_of(core * out.shape[0], 128)
            array = array.at[pl.ds(start, out.shape[0]), :]
        elif part == 1:
            start = pl.multiple_of(core * out.shape[1], 128)
            array = array.at[:, pl.ds(start, out.shape[1])]
        else:
            array = array.at[part, :]
        copies.append(pltpu.make_async_copy(array, out.at[rows, columns], sems.at[n]))
    for copy in copies:
        copy.start()
    for copy in copies:
        copy.wait()


def load(arrays, places, shape, name, limit):
    size = 2 * shape[0] * shape[1]
    return pl.pallas_call(
        functools.partial(load_kernel, places),
        in_specs=[HBM] * len(arrays),
        out_specs=VMEM,
        out_shape=pltpu.VMEM(shape, BF16),
        scratch_shapes=[pltpu.SemaphoreType.DMA((len(places),))],
        compiler_params=pltpu.CompilerParams(vmem_limit_bytes=limit * MIB),
        cost_estimate=pl.CostEstimate(flops=0, bytes_accessed=2 * size, transcendentals=0),
        name=name,
    )(*arrays)


def pack_kernel(gate, up, down, after, out, mark, held, sems):
    core = coordinates()[0]
    half = gate.shape[0] // 2
    start = (1 - core) * half
    away = pl.ds(pl.multiple_of(start, 128), half)
    takes = [
        pltpu.make_async_copy(gate.at[away, :], held.at[pl.ds(0, half), :], sems.at[0]),
        pltpu.make_async_copy(up.at[away, :], held.at[pl.ds(half, half), :], sems.at[1]),
    ]
    for n in range(half // 256):
        columns = pl.ds(pl.multiple_of(start + n * 256, 128), 256)
        rows = pl.ds(2 * half + n * 256, 256)
        takes.append(pltpu.make_async_copy(down.at[:, columns], held.at[rows, :], sems.at[2 + n]))
    gives = []
    for n in range(3):
        rows = pl.ds(n * half, half)
        gives.append(
            pltpu.make_async_copy(held.at[rows, :], out.at[rows, :], sems.at[len(takes) + n])
        )
    for take in takes:
        take.start()
    mark[...] = jnp.zeros_like(mark)
    for n, give in enumerate(gives):
        for take in takes[n : n + 1] if n < 2 else takes[2:]:
            take.wait()
        give.start()
    for give in gives:
        give.wait()


def pack(gate, up, down, after):
    half = gate.shape[0] // 2
    return pl.pallas_call(
        pack_kernel,
        in_specs=[HBM] * 3 + [pl.BlockSpec(memory_space=pl.ANY)],
        out_specs=[HBM, VMEM],
        out_shape=[jax.ShapeDtypeStruct((3 * half, 256), BF16), pltpu.VMEM((8, 128), F32)],
        scratch_shapes=[
            pltpu.VMEM((3 * half, 256), BF16),
            pltpu.SemaphoreType.DMA((5 + half // 256,)),
        ],
        compiler_params=pltpu.CompilerParams(vmem_limit_bytes=56 * MIB),
        cost_estimate=pl.CostEstimate(flops=0, bytes_accessed=12 * MIB, transcendentals=0),
        name="pack",
    )(gate, up, down, after)


def call(kernel, args, outs, name, flops, scratch=()):
    return pl.pallas_call(
        kernel,
        in_specs=[VMEM] * len(args),
        out_specs=[VMEM] * len(outs),
        out_shape=[jax.ShapeDtypeStruct(*out) for out in outs],
        scratch_shapes=list(scratch),
        compiler_params=pltpu.CompilerParams(vmem_limit_bytes=24 * MIB),
        cost_estimate=pl.CostEstimate(flops=flops, bytes_accessed=1 << 20, transcendentals=0),
        name=name,
    )(*args)


def turn_kernel(got, mark, o0, o1, o2, o3):
    rows = got[...].reshape(256, got.shape[2])
    i = iota((256, 1), 0)
    index = (i & 15) * 16 + (i >> 6) * 4 + ((i >> 4) & 3)
    rows = jnp.dot(pick(index, 256), rows, preferred_element_type=F32).astype(BF16)
    for d, out in enumerate((o0, o1, o2, o3)):
        out[...] = rows[d * 64 : d * 64 + 64]


def values_kernel(p0, p1, p2, p3, uv_own, uv_other, out):
    for head, uv in enumerate((uv_own, uv_other)):
        rows = jnp.concatenate(
            [p[head * 32 : head * 32 + 32, :] for p in (p0, p1, p2, p3)], axis=0
        )
        val = jnp.dot(rows, uv[...], preferred_element_type=F32)
        out[:, head * VHEAD : head * VHEAD + VHEAD] = val.astype(BF16)


PARTS = ((0, 64), (64, 96), (96, 128), (128, 160), (160, 192), (192, 224), (224, 256))


LATE = PARTS[:3] + PARTS[5:] + PARTS[3:5]


def put_parts(full, outs, columns, parts):
    for ref, (lo, hi) in zip(outs, parts):
        ref[:, columns] = full[lo:hi].astype(BF16)


def project_kernel(mine, theirs, w, rows, back, *refs):
    outs, val = refs[:-1], refs[-1]
    _, _, me_t, me_p = coordinates()
    i = iota((128, 1), 0)
    t, b = ((i >> 5) + me_t) & 3, i & 3
    index = ((b - me_p) & 3) * 32 + (i & 0x1C) + t
    sib = jnp.dot(pick(index, 128), theirs[...], preferred_element_type=F32).astype(BF16)
    for d in range(4):
        for s, rows in enumerate((mine[...], sib)):
            at = d * 64 + s * 32
            rows = rows[d * 32 : d * 32 + 32]
            val[at : at + 32, s * VHEAD : s * VHEAD + VHEAD] = rows[:, :VHEAD]
            val[at : at + 32, (1 - s) * VHEAD : (2 - s) * VHEAD] = rows[:, VHEAD:]
    quarter = w.shape[1] // 4
    for q in range(4):
        columns = slice(q * quarter, (q + 1) * quarter)
        full = jnp.dot(val[...], w[:, columns], preferred_element_type=F32)
        put_parts(full, outs, columns, PARTS)


def product_outs(half):
    return [((hi - lo, half), BF16) for lo, hi in PARTS]


def gate_up_kernel(*refs):
    *refs, back, w, part, sent, squares, weight = refs
    count = part.shape[0]
    first = sent.shape[0] - count
    pieces = refs
    if first:
        before, *pieces = refs
        sent[:first, :] = before[...]
    sent = sent.at[pl.ds(first, count), :]
    expert = coordinates()[1]
    half = w.shape[0]
    quarter = half // 4
    sq = jnp.zeros((count, 1), F32)
    for q in range(4):
        columns = slice(q * quarter, (q + 1) * quarter)
        a = jnp.concatenate([p[:, columns] for p in pieces], axis=0)
        share = jnp.dot(a, w[columns, :], preferred_element_type=F32)
        if q == 0:
            part[...] = share
        else:
            part[...] += share
        plain = a.astype(F32) * back[:, columns]
        sq += jnp.sum(plain * plain, axis=1, keepdims=True)
    squares[...] = sq
    sent[:, :1024] = part[...].astype(BF16)
    hi = sq.astype(BF16).astype(F32)
    mid = (sq - hi).astype(BF16).astype(F32)
    lo = sq - hi - mid
    lane = iota((count, 128), 1)
    sent[:, 1024:] = jnp.where(
        lane == 0, hi, jnp.where(lane == 1, mid, jnp.where(lane == 2, lo, 0.0))
    ).astype(BF16)
    n = jnp.concatenate([p[:, half:] for p in pieces], axis=0).astype(F32)
    high = pltpu.roll(n, 128 - TOP, 1)
    low = pltpu.roll(n, 128 - 2 * TOP, 1)
    hit = (lane < TOP) & (n == expert.astype(F32))
    weight[...] = jnp.sum(jnp.where(hit, high + low, 0.0), axis=1, keepdims=True)


def gate_up(before, pieces, back, w):
    count = sum(p.shape[0] for p in pieces)
    rows = count + sum(b.shape[0] for b in before)
    return call(
        gate_up_kernel,
        (*before, *pieces, back, w),
        [((count, 1024), F32), ((rows, 1152), BF16), ((count, 1), F32), ((count, 1), F32)],
        "gate_up",
        count << 23,
    )


def late(d):
    return d ^ (d >> 1)


def down_kernel(p0, q0, w0, p1, q1, w1, got, w, *refs):
    outs, hidden = refs[:-1], refs[-1]
    _, _, me_t, me_p = coordinates()
    i = iota((256, 1), 0)
    d, s, rest = late(i >> 6), (i >> 5) & 1, i & 0x1C
    t, b = (d + me_t) & 3, i & 3
    index = late((b - me_p) & 3) * 64 + (1 - s) * 32 + rest + t
    theirs = jnp.dot(pick(index, 256), got[...], preferred_element_type=F32)
    at = 0
    for part, squares in ((p0, q0), (p1, q1)):
        rows = slice(at, at + part.shape[0])
        at += part.shape[0]
        tail = theirs[rows, 1024:]
        lane = iota(tail.shape, 1)
        sq = squares[...] + jnp.sum(jnp.where(lane < 3, tail, 0.0), axis=1, keepdims=True)
        scale = lax.rsqrt(sq / 7168.0 + 1e-06)
        for block in range(2):
            left, right = block * 512, 512 - block * 512
            gate = (part[:, left : left + 256] + theirs[rows, right : right + 256]) * scale
            left, right = left + 256, right + 256
            up = (part[:, left : left + 256] + theirs[rows, right : right + 256]) * scale
            hidden[rows, block * 256 : block * 256 + 256] = (
                gate / (1.0 + jnp.exp(-gate)) * up
            ).astype(BF16)
    weight = jnp.concatenate([w0[...], w1[...]], axis=0)
    quarter = w.shape[1] // 4
    for q in range(4):
        columns = slice(q * quarter, (q + 1) * quarter)
        full = jnp.dot(hidden[...], w[:, columns], preferred_element_type=F32)
        put_parts(full * weight, outs, columns, LATE)


def add(a, b):
    return (a.astype(F32) + b.astype(F32)).astype(BF16)


def reduce_rows(b0, b1t, b1b, b2t, b2b, b3t, b3b):
    far_left, far_right = ahead(b2t, 1), ahead(b2b, -1)
    left_b, right_t = ahead(b1b, 1), ahead(b3t, -1)
    left_t, right_b = ahead(add(b1t, far_left), 1), ahead(add(b3b, far_right), -1)
    left = jnp.concatenate([left_t, left_b])
    right = jnp.concatenate([right_t, right_b])
    mine = (b0.astype(F32) + left.astype(F32) + right.astype(F32)).astype(BF16)
    mine = mine.reshape(4, 16, mine.shape[1]).swapaxes(0, 1)
    return jnp.sum(plane(mine).astype(F32), axis=0)


def gather_rows(a):
    a0 = plane(jnp.broadcast_to(a, (16, *a.shape)))
    a0 = a0.swapaxes(0, 1).reshape(64, a.shape[1])
    top, bottom = a0[:32], a0[32:]
    left_t, right_b = ahead(top, 1), ahead(bottom, -1)
    left_b, right_t = ahead(bottom, 1), ahead(top, -1)
    return (a0, right_t, right_b, left_t, left_b), (ahead(left_t, 1), ahead(right_b, -1))


def shards(queries, cache, lengths, w_uv, w_out, residual, gain, ids, gates, w_gate, w_up, w_down):
    me = lax.axis_index(AXES)
    core = (me ^ (me >> 1) ^ (me >> 3)) & 1
    half = residual.shape[1] // 2

    def own(w, axis):
        return lax.dynamic_slice_in_dim(w, core * half, half, axis)

    def away(w, axis):
        return lax.dynamic_slice_in_dim(w, (1 - core) * half, half, axis)

    sent, out_other = attend(lengths, queries.swapaxes(1, 2), cache.swapaxes(1, 2), w_out)
    uv_other = swap(w_uv[0])
    packed, mark = pack(w_gate[0], w_up[0], w_down[0], out_other)
    blocks = pl.pallas_call(
        turn_kernel,
        in_specs=[VMEM, VMEM],
        out_specs=[VMEM] * 4,
        out_shape=[jax.ShapeDtypeStruct((64, LATENT), BF16)] * 4,
        compiler_params=pltpu.CompilerParams(vmem_limit_bytes=16 * MIB),
        name="turn",
    )(plane(sent), mark)
    blocks = exchange(blocks)
    out_other = swap(out_other)
    every = slice(None)
    w_out = load(
        (w_out, out_other),
        ((0, 1, slice(0, VHEAD), every), (1, every, slice(VHEAD, 2 * VHEAD), every)),
        (2 * VHEAD, half),
        "load_out",
        8,
    )
    (mine,) = call(
        values_kernel,
        (*blocks, w_uv[0], uv_other),
        [((128, 2 * VHEAD), BF16)],
        "values",
        1 << 25,
    )
    packed = swap(packed)

    gates_hi = gates.astype(BF16)
    gates_lo = (gates - gates_hi.astype(F32)).astype(BF16)
    names = jnp.concatenate(
        [ids.astype(BF16), gates_hi, gates_lo, jnp.zeros((2, 128 - 3 * TOP), BF16)], axis=1
    )
    rows = jnp.concatenate(
        [
            jnp.concatenate([own(residual, 1), names], axis=1),
            swap(jnp.concatenate([away(residual, 1), names], axis=1)),
        ]
    )
    res, names = rows[:, :half].astype(F32), rows[:, half:]
    back = (1.0 / own(gain, 0)).reshape(1, half)

    pieces = call(
        project_kernel,
        (mine, swap(mine), w_out, rows, back),
        product_outs(half),
        "project",
        1 << 29,
        [pltpu.VMEM((256, 2 * VHEAD), BF16)],
    )
    mixed = res + reduce_rows(*pieces)

    scaled = (mixed * own(gain, 0)).astype(BF16)
    w_gu = load(
        (w_gate[0], w_up[0], packed),
        (
            (0, 0, every, slice(0, 256)),
            (1, 0, every, slice(256, 512)),
            (2, slice(0, half), every, slice(512, 768)),
            (2, slice(half, 2 * half), every, slice(768, 1024)),
        ),
        (half, 1024),
        "load_gate_up",
        42,
    )
    near, far = gather_rows(jnp.concatenate([scaled, names], axis=1))
    p0, sent, q0, w0 = gate_up((), near, back, w_gu)
    p1, sent, q1, w1 = gate_up((sent,), far, back, w_gu)
    w_down = load(
        (w_down[0], packed),
        (
            (0, 1, slice(0, 256), every),
            *(
                (1, slice(2 * half + n, 2 * half + n + 256), slice(256, 512), slice(n, n + 256))
                for n in range(0, half, 256)
            ),
        ),
        (512, half),
        "load_down",
        46,
    )
    pieces = call(
        down_kernel,
        (p0, q0, w0, p1, q1, w1, swap(sent), w_down),
        product_outs(half),
        "down",
        1 << 30,
        [pltpu.VMEM((256, 512), BF16)],
    )
    result = (mixed + reduce_rows(*pieces)).astype(BF16)

    mine, other = result[:2], swap(result[2:])
    return jnp.where(
        core == 0, jnp.concatenate([mine, other], 1), jnp.concatenate([other, mine], 1)
    )


def solution(mesh):
    in_specs = (
        P(("grp", "dev"), None, None),
        P(("grp", "dev"), None, None),
        P(("grp", "dev")),
        P(("grp", "dev"), None, None),
        P(("grp", "dev"), None),
        P(("grp", "dev"), None),
        P(),
        P(("grp", "dev"), None),
        P(("grp", "dev"), None),
        P(("grp", "dev"), None, None),
        P(("grp", "dev"), None, None),
        P(("grp", "dev"), None, None),
    )
    out_specs = P(("grp", "dev"), None)
    return jax.shard_map(shards, mesh=mesh, in_specs=in_specs, out_specs=out_specs, check_vma=False)
```

```python
import functools

import jax
import jax.numpy as jnp
from jax import lax
from jax.experimental import pallas as pl
from jax.experimental.pallas import tpu as pltpu
from jax.sharding import PartitionSpec as P

LATENT = 512
VHEAD = 128
TOP = 8
AXES = ("grp", "dev")
F32 = jnp.float32
BF16 = jnp.bfloat16
I32 = jnp.int32
MIB = 1 << 20
CHUNK = 1024

softmax_scale = 192.0 ** (-0.5)


def device(y, z, x, c):
    return ((y * 4 + z) * 4 + x) * 2 + (c ^ ((x + z) & 1))


RINGS = [[device(y, z, x, 0) for x in range(4)] for y in range(4) for z in range(4)] + [
    [device(y, z, x, 1) for z in range(4)] for y in range(4) for x in range(4)
]
PLANES = [[device(y, z, x, 0) for y in range(4) for z in range(4)] for x in range(4)] + [
    [device(y, z, x, 1) for y in range(4) for x in range(4)] for z in range(4)
]
SIBLING = [(i, i ^ 1) for i in range(128)]


def swap(a):
    return lax.ppermute(a, AXES, SIBLING)


def ahead(a, step):
    return lax.ppermute(a, AXES, [(r[i], r[(i + step) % 4]) for r in RINGS for i in range(4)])


def plane(a):
    return lax.all_to_all(a, AXES, 0, 0, axis_index_groups=PLANES, tiled=True)


def exchange(blocks):
    far = ahead(blocks[2], 2)
    return [blocks[0], ahead(blocks[3], 3), far, ahead(blocks[1], 1)]


def iota(shape, axis):
    return lax.broadcasted_iota(I32, shape, axis)


def pick(index, count):
    return jnp.where(index == iota((index.shape[0], count), 1), 1.0, 0.0).astype(BF16)


def coordinates():
    me = lax.axis_index("grp") * 64 + lax.axis_index("dev")
    z, x = (me >> 3) & 3, (me >> 1) & 3
    core = (me ^ x ^ z) & 1
    return core, me >> 2, jnp.where(core == 0, x, z), jnp.where(core == 0, z, x)


HBM = pl.BlockSpec(memory_space=pltpu.HBM)
VMEM = pl.BlockSpec(memory_space=pltpu.VMEM)


def attend_kernel(
    lens, query, cache, w_out, sent, out_other, q, kv, peak, total, acc, both, held, sems, kv_sems
):
    core, _, me_t, _ = coordinates()
    half = held.shape[1]
    away = pl.ds(pl.multiple_of((1 - core) * half, 128), half)
    take = pltpu.make_async_copy(w_out.at[:, away], held, sems.at[0])
    give = pltpu.make_async_copy(held, out_other, sems.at[1])
    ask = pltpu.make_async_copy(query, q, sems.at[2])

    def chunk(r, j):
        slots = pl.ds(pl.multiple_of(j * CHUNK, CHUNK), CHUNK)
        return pltpu.make_async_copy(cache.at[r, :, slots], kv.at[r, j], kv_sems.at[r, j])

    live = [(lens[r] + CHUNK - 1) // CHUNK for r in range(2)]
    ask.start()
    for r in range(2):

        @pl.loop(0, live[r])
        def _(j, r=r):
            chunk(r, j).start()

    take.start()
    ask.wait()
    for r in range(2):
        heads = lax.dot_general(
            pick(iota((128, 1), 0), 128), q[r], (((1,), (1,)), ((), ())), preferred_element_type=F32
        ).astype(BF16)
        peak[...] = jnp.full_like(peak, -1e30)
        total[...] = jnp.zeros_like(total)
        acc[...] = jnp.zeros_like(acc)

        @pl.loop(0, live[r])
        def _(j, r=r, heads=heads):
            chunk(r, j).wait()
            score = jnp.dot(heads, kv[r, j], preferred_element_type=F32)
            place = j * CHUNK + iota(score.shape, 1)
            score = jnp.where(place < lens[r], score * softmax_scale, -1e30)
            before = peak[...]
            now = jnp.maximum(before, jnp.max(score, axis=1, keepdims=True))
            fade = jnp.exp(before - now)
            weight = jnp.exp(score - now)
            peak[...] = now
            total[...] = total[...] * fade + jnp.sum(weight, axis=1, keepdims=True)
            acc[...] = acc[...] * fade + lax.dot_general(
                weight.astype(BF16),
                kv[r, j, :LATENT, :],
                (((1,), (1,)), ((), ())),
                preferred_element_type=F32,
            )

        both[r * 128 : r * 128 + 128, :] = (acc[...] / total[...]).astype(BF16)
        if r == 0:
            take.wait()
            give.start()

    i = iota((256, 1), 0)
    y, b, t = i >> 6, (i >> 4) & 3, (me_t + (i >> 2)) & 3
    z = jnp.where(core == 0, b, t)
    x = jnp.where(core == 0, t, b)
    head = device(y, z, x, ((i >> 1) & 1) ^ core)
    rows = jnp.dot(pick((i & 1) * 128 + head, 256), both[...], preferred_element_type=F32)
    sent[...] = rows.astype(BF16).reshape(sent.shape)
    give.wait()


def attend(lengths, queries, cache, w_out):
    _, size, heads = queries.shape
    half = w_out.shape[1] // 2
    chunks = cache.shape[2] // CHUNK
    return pl.pallas_call(
        attend_kernel,
        in_specs=[pl.BlockSpec(memory_space=pltpu.SMEM), HBM, HBM, HBM],
        out_specs=[VMEM, HBM],
        out_shape=[
            pltpu.VMEM((16, 16, LATENT), BF16),
            jax.ShapeDtypeStruct((VHEAD, half), BF16),
        ],
        scratch_shapes=[
            pltpu.VMEM((2, size, heads), BF16),
            pltpu.VMEM((2, chunks, size, CHUNK), BF16),
            pltpu.VMEM((heads, 1), F32),
            pltpu.VMEM((heads, 1), F32),
            pltpu.VMEM((heads, LATENT), F32),
            pltpu.VMEM((2 * heads, LATENT), BF16),
            pltpu.VMEM((VHEAD, half), BF16),
            pltpu.SemaphoreType.DMA((3,)),
            pltpu.SemaphoreType.DMA((2, chunks)),
        ],
        compiler_params=pltpu.CompilerParams(vmem_limit_bytes=56 * MIB),
        name="attend",
    )(lengths, queries, cache, w_out)


def load_kernel(places, *refs):
    *arrays, out, sems = refs
    core = coordinates()[0]
    copies = []
    for n, (which, part, at, size) in enumerate(places):
        axis, start = part
        if axis is not None:
            start = pl.multiple_of(core * out.shape[axis] + start, 128)
        if axis == 1:
            array = arrays[which].at[:, pl.ds(start, size[1])]
        else:
            array = arrays[which].at[pl.ds(start, size[0]), :]
        spot = out.at[pl.ds(at[0], size[0]), pl.ds(at[1], size[1])]
        copies.append(pltpu.make_async_copy(array, spot, sems.at[n]))
    for copy in copies:
        copy.start()
    for copy in copies:
        copy.wait()


def load(arrays, places, shape, name, limit):
    size = 2 * shape[0] * shape[1]
    return pl.pallas_call(
        functools.partial(load_kernel, places),
        in_specs=[HBM] * len(arrays),
        out_specs=VMEM,
        out_shape=pltpu.VMEM(shape, BF16),
        scratch_shapes=[pltpu.SemaphoreType.DMA((len(places),))],
        compiler_params=pltpu.CompilerParams(vmem_limit_bytes=limit * MIB),
        cost_estimate=pl.CostEstimate(flops=0, bytes_accessed=2 * size, transcendentals=0),
        name=name,
    )(*arrays)


def pack_kernel(gate, up, down, after, out, mark, held, sems):
    core = coordinates()[0]
    half = gate.shape[0] // 2
    start = (1 - core) * half
    away = pl.ds(pl.multiple_of(start, 128), half)
    takes = [
        pltpu.make_async_copy(gate.at[away, :], held.at[pl.ds(0, half), :], sems.at[0]),
        pltpu.make_async_copy(up.at[away, :], held.at[pl.ds(half, half), :], sems.at[1]),
    ]
    for n in range(half // 256):
        columns = pl.ds(pl.multiple_of(start + n * 256, 128), 256)
        rows = pl.ds(2 * half + n * 256, 256)
        takes.append(pltpu.make_async_copy(down.at[:, columns], held.at[rows, :], sems.at[2 + n]))
    gives = []
    for n in range(3):
        rows = pl.ds(n * half, half)
        gives.append(
            pltpu.make_async_copy(held.at[rows, :], out.at[rows, :], sems.at[len(takes) + n])
        )
    for take in takes:
        take.start()
    mark[...] = jnp.zeros_like(mark)
    for n, give in enumerate(gives):
        for take in takes[n : n + 1] if n < 2 else takes[2:]:
            take.wait()
        give.start()
    for give in gives:
        give.wait()


def pack(gate, up, down, after):
    half = gate.shape[0] // 2
    return pl.pallas_call(
        pack_kernel,
        in_specs=[HBM] * 3 + [pl.BlockSpec(memory_space=pl.ANY)],
        out_specs=[HBM, VMEM],
        out_shape=[jax.ShapeDtypeStruct((3 * half, 256), BF16), pltpu.VMEM((8, 128), F32)],
        scratch_shapes=[
            pltpu.VMEM((3 * half, 256), BF16),
            pltpu.SemaphoreType.DMA((5 + half // 256,)),
        ],
        compiler_params=pltpu.CompilerParams(vmem_limit_bytes=56 * MIB),
        cost_estimate=pl.CostEstimate(flops=0, bytes_accessed=12 * MIB, transcendentals=0),
        name="pack",
    )(gate, up, down, after)


def call(kernel, args, outs, name, flops, scratch=()):
    return pl.pallas_call(
        kernel,
        in_specs=[VMEM] * len(args),
        out_specs=[VMEM] * len(outs),
        out_shape=[jax.ShapeDtypeStruct(*out) for out in outs],
        scratch_shapes=list(scratch),
        compiler_params=pltpu.CompilerParams(vmem_limit_bytes=24 * MIB),
        cost_estimate=pl.CostEstimate(flops=flops, bytes_accessed=1 << 20, transcendentals=0),
        name=name,
    )(*args)


def turn_kernel(got, mark, o0, o1, o2, o3):
    rows = got[...].reshape(256, got.shape[2])
    i = iota((256, 1), 0)
    index = (i & 15) * 16 + (i >> 6) * 4 + ((i >> 4) & 3)
    rows = jnp.dot(pick(index, 256), rows, preferred_element_type=F32).astype(BF16)
    for d, out in enumerate((o0, o1, o2, o3)):
        out[...] = rows[d * 64 : d * 64 + 64]


def values_kernel(p0, p1, p2, p3, uv_own, uv_other, out):
    for head, uv in enumerate((uv_own, uv_other)):
        rows = jnp.concatenate(
            [p[head * 32 : head * 32 + 32, :] for p in (p0, p1, p2, p3)], axis=0
        )
        val = jnp.dot(rows, uv[...], preferred_element_type=F32)
        out[:, head * VHEAD : head * VHEAD + VHEAD] = val.astype(BF16)


PARTS = ((0, 64), (64, 96), (96, 128), (128, 160), (160, 192), (192, 224), (224, 256))


LATE = PARTS[:3] + PARTS[5:] + PARTS[3:5]


def put_parts(full, outs, columns, parts):
    for ref, (lo, hi) in zip(outs, parts):
        ref[:, columns] = full[lo:hi].astype(BF16)


def project_kernel(mine, theirs, w, *refs):
    outs, val = refs[:-1], refs[-1]
    _, _, me_t, me_p = coordinates()
    i = iota((128, 1), 0)
    t, b = ((i >> 5) + me_t) & 3, i & 3
    index = ((b - me_p) & 3) * 32 + (i & 0x1C) + t
    sib = jnp.dot(pick(index, 128), theirs[...], preferred_element_type=F32).astype(BF16)
    for d in range(4):
        for s, rows in enumerate((mine[...], sib)):
            at = d * 64 + s * 32
            rows = rows[d * 32 : d * 32 + 32]
            val[at : at + 32, s * VHEAD : s * VHEAD + VHEAD] = rows[:, :VHEAD]
            val[at : at + 32, (1 - s) * VHEAD : (2 - s) * VHEAD] = rows[:, VHEAD:]
    quarter = w.shape[1] // 4
    for q in range(4):
        columns = slice(q * quarter, (q + 1) * quarter)
        full = jnp.dot(val[...], w[:, columns], preferred_element_type=F32)
        put_parts(full, outs, columns, PARTS)


def product_outs(half):
    return [((hi - lo, half), BF16) for lo, hi in PARTS]


def gate_up_kernel(*refs):
    *refs, back, w, part, sent, squares, weight = refs
    count = part.shape[0]
    first = sent.shape[0] - count
    pieces = refs
    if first:
        before, *pieces = refs
        sent[:first, :] = before[...]
    sent = sent.at[pl.ds(first, count), :]
    expert = coordinates()[1]
    half = w.shape[0]
    quarter = half // 4
    sq = jnp.zeros((count, 1), F32)
    for q in range(4):
        columns = slice(q * quarter, (q + 1) * quarter)
        a = jnp.concatenate([p[:, columns] for p in pieces], axis=0)
        share = jnp.dot(a, w[columns, :], preferred_element_type=F32)
        if q == 0:
            part[...] = share
        else:
            part[...] += share
        plain = a.astype(F32) * back[:, columns]
        sq += jnp.sum(plain * plain, axis=1, keepdims=True)
    squares[...] = sq
    sent[:, :1024] = part[...].astype(BF16)
    hi = sq.astype(BF16).astype(F32)
    mid = (sq - hi).astype(BF16).astype(F32)
    lo = sq - hi - mid
    lane = iota((count, 128), 1)
    sent[:, 1024:] = jnp.where(
        lane == 0, hi, jnp.where(lane == 1, mid, jnp.where(lane == 2, lo, 0.0))
    ).astype(BF16)
    n = jnp.concatenate([p[:, half:] for p in pieces], axis=0).astype(F32)
    high = pltpu.roll(n, 128 - TOP, 1)
    low = pltpu.roll(n, 128 - 2 * TOP, 1)
    hit = (lane < TOP) & (n == expert.astype(F32))
    weight[...] = jnp.sum(jnp.where(hit, high + low, 0.0), axis=1, keepdims=True)


def gate_up(before, pieces, back, w):
    count = sum(p.shape[0] for p in pieces)
    rows = count + sum(b.shape[0] for b in before)
    return call(
        gate_up_kernel,
        (*before, *pieces, back, w),
        [((count, 1024), F32), ((rows, 1152), BF16), ((count, 1), F32), ((count, 1), F32)],
        "gate_up",
        count << 23,
    )


def late(d):
    return d ^ (d >> 1)


def down_kernel(p0, q0, w0, p1, q1, w1, got, w, *refs):
    outs, hidden = refs[:-1], refs[-1]
    _, _, me_t, me_p = coordinates()
    i = iota((256, 1), 0)
    d, s, rest = late(i >> 6), (i >> 5) & 1, i & 0x1C
    t, b = (d + me_t) & 3, i & 3
    index = late((b - me_p) & 3) * 64 + (1 - s) * 32 + rest + t
    theirs = jnp.dot(pick(index, 256), got[...], preferred_element_type=F32)
    at = 0
    for part, squares in ((p0, q0), (p1, q1)):
        rows = slice(at, at + part.shape[0])
        at += part.shape[0]
        tail = theirs[rows, 1024:]
        lane = iota(tail.shape, 1)
        sq = squares[...] + jnp.sum(jnp.where(lane < 3, tail, 0.0), axis=1, keepdims=True)
        scale = lax.rsqrt(sq / 7168.0 + 1e-06)
        for block in range(2):
            left, right = block * 512, 512 - block * 512
            gate = (part[:, left : left + 256] + theirs[rows, right : right + 256]) * scale
            left, right = left + 256, right + 256
            up = (part[:, left : left + 256] + theirs[rows, right : right + 256]) * scale
            hidden[rows, block * 256 : block * 256 + 256] = (
                gate / (1.0 + jnp.exp(-gate)) * up
            ).astype(BF16)
    weight = jnp.concatenate([w0[...], w1[...]], axis=0)
    quarter = w.shape[1] // 4
    for q in range(4):
        columns = slice(q * quarter, (q + 1) * quarter)
        full = jnp.dot(hidden[...], w[:, columns], preferred_element_type=F32)
        put_parts(full * weight, outs, columns, LATE)


def add(a, b):
    return (a.astype(F32) + b.astype(F32)).astype(BF16)


def reduce_rows(b0, b1t, b1b, b2t, b2b, b3t, b3b):
    far_left, far_right = ahead(b2t, 1), ahead(b2b, -1)
    left_b, right_t = ahead(b1b, 1), ahead(b3t, -1)
    left_t, right_b = ahead(add(b1t, far_left), 1), ahead(add(b3b, far_right), -1)
    left = jnp.concatenate([left_t, left_b])
    right = jnp.concatenate([right_t, right_b])
    mine = (b0.astype(F32) + left.astype(F32) + right.astype(F32)).astype(BF16)
    mine = mine.reshape(4, 16, mine.shape[1]).swapaxes(0, 1)
    return jnp.sum(plane(mine).astype(F32), axis=0)


def gather_rows(a):
    a0 = plane(jnp.broadcast_to(a, (16, *a.shape)))
    a0 = a0.swapaxes(0, 1).reshape(64, a.shape[1])
    top, bottom = a0[:32], a0[32:]
    left_t, right_b = ahead(top, 1), ahead(bottom, -1)
    left_b, right_t = ahead(bottom, 1), ahead(top, -1)
    return (a0, right_t, right_b, left_t, left_b), (ahead(left_t, 1), ahead(right_b, -1))


def shards(queries, cache, lengths, w_uv, w_out, residual, gain, ids, gates, w_gate, w_up, w_down):
    me = lax.axis_index(AXES)
    core = (me ^ (me >> 1) ^ (me >> 3)) & 1
    half = residual.shape[1] // 2

    def own(w, axis):
        return lax.dynamic_slice_in_dim(w, core * half, half, axis)

    def away(w, axis):
        return lax.dynamic_slice_in_dim(w, (1 - core) * half, half, axis)

    sent, out_other = attend(lengths, queries.swapaxes(1, 2), cache.swapaxes(1, 2), w_out)
    uv_other = swap(w_uv[0])
    packed, mark = pack(w_gate[0], w_up[0], w_down[0], out_other)
    blocks = pl.pallas_call(
        turn_kernel,
        in_specs=[VMEM, VMEM],
        out_specs=[VMEM] * 4,
        out_shape=[jax.ShapeDtypeStruct((64, LATENT), BF16)] * 4,
        compiler_params=pltpu.CompilerParams(vmem_limit_bytes=16 * MIB),
        name="turn",
    )(plane(sent), mark)
    blocks = exchange(blocks)
    out_other = swap(out_other)
    quarter = half // 4
    w_out = load(
        (w_out, out_other),
        (
            *((0, (1, n), (0, n), (VHEAD, quarter)) for n in range(0, half, quarter)),
            (1, (None, 0), (VHEAD, 0), (VHEAD, half)),
        ),
        (2 * VHEAD, half),
        "load_out",
        8,
    )
    (mine,) = call(
        values_kernel,
        (*blocks, w_uv[0], uv_other),
        [((128, 2 * VHEAD), BF16)],
        "values",
        1 << 25,
    )
    packed = swap(packed)

    gates_hi = gates.astype(BF16)
    gates_lo = (gates - gates_hi.astype(F32)).astype(BF16)
    names = jnp.concatenate(
        [ids.astype(BF16), gates_hi, gates_lo, jnp.zeros((2, 128 - 3 * TOP), BF16)], axis=1
    )
    rows = jnp.concatenate(
        [
            jnp.concatenate([own(residual, 1), names], axis=1),
            swap(jnp.concatenate([away(residual, 1), names], axis=1)),
        ]
    )
    res, names = rows[:, :half].astype(F32), rows[:, half:]

    pieces = call(
        project_kernel,
        (mine, swap(mine), w_out),
        product_outs(half),
        "project",
        1 << 29,
        [pltpu.VMEM((256, 2 * VHEAD), BF16)],
    )
    mixed = res + reduce_rows(*pieces)

    scaled = (mixed * own(gain, 0)).astype(BF16)
    w_gu = load(
        (w_gate[0], w_up[0], packed),
        tuple(
            place
            for n in range(0, half, quarter)
            for place in (
                (0, (0, n), (n, 0), (quarter, 256)),
                (1, (0, n), (n, 256), (quarter, 256)),
                (2, (None, n), (n, 512), (quarter, 256)),
                (2, (None, half + n), (n, 768), (quarter, 256)),
            )
        ),
        (half, 1024),
        "load_gate_up",
        42,
    )
    near, far = gather_rows(jnp.concatenate([scaled, names], axis=1))
    back = (1.0 / own(gain, 0)).reshape(1, half)
    p0, sent, q0, w0 = gate_up((), near, back, w_gu)
    p1, sent, q1, w1 = gate_up((sent,), far, back, w_gu)
    w_down = load(
        (w_down[0], packed),
        (
            *((0, (1, n), (0, n), (256, quarter)) for n in range(0, half, quarter)),
            *((1, (None, 2 * half + n), (256, n), (256, 256)) for n in range(0, half, 256)),
        ),
        (512, half),
        "load_down",
        46,
    )
    pieces = call(
        down_kernel,
        (p0, q0, w0, p1, q1, w1, swap(sent), w_down),
        product_outs(half),
        "down",
        1 << 30,
        [pltpu.VMEM((256, 512), BF16)],
    )
    result = (mixed + reduce_rows(*pieces)).astype(BF16)

    mine, other = result[:2], swap(result[2:])
    return jnp.where(
        core == 0, jnp.concatenate([mine, other], 1), jnp.concatenate([other, mine], 1)
    )


def solution(mesh):
    in_specs = (
        P(("grp", "dev"), None, None),
        P(("grp", "dev"), None, None),
        P(("grp", "dev")),
        P(("grp", "dev"), None, None),
        P(("grp", "dev"), None),
        P(("grp", "dev"), None),
        P(),
        P(("grp", "dev"), None),
        P(("grp", "dev"), None),
        P(("grp", "dev"), None, None),
        P(("grp", "dev"), None, None),
        P(("grp", "dev"), None, None),
    )
    out_specs = P(("grp", "dev"), None)
    return jax.shard_map(shards, mesh=mesh, in_specs=in_specs, out_specs=out_specs, check_vma=False)
```

```python
import functools

import jax
import jax.numpy as jnp
from jax import lax
from jax.experimental import pallas as pl
from jax.experimental.pallas import tpu as pltpu
from jax.sharding import PartitionSpec as P

LATENT = 512
VHEAD = 128
TOP = 8
AXES = ("grp", "dev")
F32 = jnp.float32
BF16 = jnp.bfloat16
I32 = jnp.int32
MIB = 1 << 20
CHUNK = 1024

softmax_scale = 192.0 ** (-0.5)


def device(y, z, x, c):
    return ((y * 4 + z) * 4 + x) * 2 + (c ^ ((x + z) & 1))


RINGS = [[device(y, z, x, 0) for x in range(4)] for y in range(4) for z in range(4)] + [
    [device(y, z, x, 1) for z in range(4)] for y in range(4) for x in range(4)
]
PLANES = [[device(y, z, x, 0) for y in range(4) for z in range(4)] for x in range(4)] + [
    [device(y, z, x, 1) for y in range(4) for x in range(4)] for z in range(4)
]
SIBLING = [(i, i ^ 1) for i in range(128)]


def swap(a):
    return lax.ppermute(a, AXES, SIBLING)


def ahead(a, step):
    return lax.ppermute(a, AXES, [(r[i], r[(i + step) % 4]) for r in RINGS for i in range(4)])


def plane(a):
    return lax.all_to_all(a, AXES, 0, 0, axis_index_groups=PLANES, tiled=True)


def exchange(blocks):
    far = ahead(blocks[2], 2)
    return [blocks[0], ahead(blocks[3], 3), far, ahead(blocks[1], 1)]


def iota(shape, axis):
    return lax.broadcasted_iota(I32, shape, axis)


def pick(index, count):
    return jnp.where(index == iota((index.shape[0], count), 1), 1.0, 0.0).astype(BF16)


def coordinates():
    me = lax.axis_index("grp") * 64 + lax.axis_index("dev")
    z, x = (me >> 3) & 3, (me >> 1) & 3
    core = (me ^ x ^ z) & 1
    return core, me >> 2, jnp.where(core == 0, x, z), jnp.where(core == 0, z, x)


HBM = pl.BlockSpec(memory_space=pltpu.HBM)
VMEM = pl.BlockSpec(memory_space=pltpu.VMEM)


def attend_kernel(
    lens, query, cache, w_out, sent, out_other, q, kv, peak, total, acc, both, held, sems, kv_sems
):
    core, _, me_t, _ = coordinates()
    half = held.shape[1]
    away = pl.ds(pl.multiple_of((1 - core) * half, 128), half)
    take = pltpu.make_async_copy(w_out.at[:, away], held, sems.at[0])
    give = pltpu.make_async_copy(held, out_other, sems.at[1])
    ask = pltpu.make_async_copy(query, q, sems.at[2])

    def chunk(r, j):
        slots = pl.ds(pl.multiple_of(j * CHUNK, CHUNK), CHUNK)
        return pltpu.make_async_copy(cache.at[r, :, slots], kv.at[r, j], kv_sems.at[r, j])

    live = [(lens[r] + CHUNK - 1) // CHUNK for r in range(2)]
    ask.start()
    for r in range(2):

        @pl.loop(0, live[r])
        def _(j, r=r):
            chunk(r, j).start()

    take.start()
    ask.wait()
    for r in range(2):
        heads = lax.dot_general(
            pick(iota((128, 1), 0), 128), q[r], (((1,), (1,)), ((), ())), preferred_element_type=F32
        ).astype(BF16)
        peak[...] = jnp.full_like(peak, -1e30)
        total[...] = jnp.zeros_like(total)
        acc[...] = jnp.zeros_like(acc)

        @pl.loop(0, live[r])
        def _(j, r=r, heads=heads):
            chunk(r, j).wait()
            score = jnp.dot(heads, kv[r, j], preferred_element_type=F32)
            place = j * CHUNK + iota(score.shape, 1)
            score = jnp.where(place < lens[r], score * softmax_scale, -1e30)
            before = peak[...]
            now = jnp.maximum(before, jnp.max(score, axis=1, keepdims=True))
            fade = jnp.exp(before - now)
            weight = jnp.exp(score - now)
            peak[...] = now
            total[...] = total[...] * fade + jnp.sum(weight, axis=1, keepdims=True)
            acc[...] = acc[...] * fade + lax.dot_general(
                weight.astype(BF16),
                kv[r, j, :LATENT, :],
                (((1,), (1,)), ((), ())),
                preferred_element_type=F32,
            )

        both[r * 128 : r * 128 + 128, :] = (acc[...] / total[...]).astype(BF16)
        if r == 0:
            take.wait()
            give.start()

    i = iota((256, 1), 0)
    y, b, t = i >> 6, (i >> 4) & 3, (me_t + (i >> 2)) & 3
    z = jnp.where(core == 0, b, t)
    x = jnp.where(core == 0, t, b)
    head = device(y, z, x, ((i >> 1) & 1) ^ core)
    rows = jnp.dot(pick((i & 1) * 128 + head, 256), both[...], preferred_element_type=F32)
    sent[...] = rows.astype(BF16).reshape(sent.shape)
    give.wait()


def attend(lengths, queries, cache, w_out):
    _, size, heads = queries.shape
    half = w_out.shape[1] // 2
    chunks = cache.shape[2] // CHUNK
    return pl.pallas_call(
        attend_kernel,
        in_specs=[pl.BlockSpec(memory_space=pltpu.SMEM), HBM, HBM, HBM],
        out_specs=[VMEM, HBM],
        out_shape=[
            pltpu.VMEM((16, 16, LATENT), BF16),
            jax.ShapeDtypeStruct((VHEAD, half), BF16),
        ],
        scratch_shapes=[
            pltpu.VMEM((2, size, heads), BF16),
            pltpu.VMEM((2, chunks, size, CHUNK), BF16),
            pltpu.VMEM((heads, 1), F32),
            pltpu.VMEM((heads, 1), F32),
            pltpu.VMEM((heads, LATENT), F32),
            pltpu.VMEM((2 * heads, LATENT), BF16),
            pltpu.VMEM((VHEAD, half), BF16),
            pltpu.SemaphoreType.DMA((3,)),
            pltpu.SemaphoreType.DMA((2, chunks)),
        ],
        compiler_params=pltpu.CompilerParams(vmem_limit_bytes=56 * MIB),
        name="attend",
    )(lengths, queries, cache, w_out)


def load_kernel(places, *refs):
    *arrays, out, sems = refs
    core = coordinates()[0]
    copies = []
    for n, (which, part, rows, columns) in enumerate(places):
        array = arrays[which]
        if part == 0:
            start = pl.multiple_of(core * out.shape[0], 128)
            array = array.at[pl.ds(start, out.shape[0]), :]
        elif part == 1:
            start = pl.multiple_of(core * out.shape[1], 128)
            array = array.at[:, pl.ds(start, out.shape[1])]
        else:
            array = array.at[part, :]
        copies.append(pltpu.make_async_copy(array, out.at[rows, columns], sems.at[n]))
    for copy in copies:
        copy.start()
    for copy in copies:
        copy.wait()


def load(arrays, places, shape, name, limit):
    size = 2 * shape[0] * shape[1]
    return pl.pallas_call(
        functools.partial(load_kernel, places),
        in_specs=[HBM] * len(arrays),
        out_specs=VMEM,
        out_shape=pltpu.VMEM(shape, BF16),
        scratch_shapes=[pltpu.SemaphoreType.DMA((len(places),))],
        compiler_params=pltpu.CompilerParams(vmem_limit_bytes=limit * MIB),
        cost_estimate=pl.CostEstimate(flops=0, bytes_accessed=2 * size, transcendentals=0),
        name=name,
    )(*arrays)


def pack_kernel(gate, up, down, after, out, mark, held, sems):
    core = coordinates()[0]
    half = gate.shape[0] // 2
    start = (1 - core) * half
    away = pl.ds(pl.multiple_of(start, 128), half)
    takes = [
        pltpu.make_async_copy(gate.at[away, :], held.at[pl.ds(0, half), :], sems.at[0]),
        pltpu.make_async_copy(up.at[away, :], held.at[pl.ds(half, half), :], sems.at[1]),
    ]
    for n in range(half // 256):
        columns = pl.ds(pl.multiple_of(start + n * 256, 128), 256)
        rows = pl.ds(2 * half + n * 256, 256)
        takes.append(pltpu.make_async_copy(down.at[:, columns], held.at[rows, :], sems.at[2 + n]))
    gives = []
    for n in range(3):
        rows = pl.ds(n * half, half)
        gives.append(
            pltpu.make_async_copy(held.at[rows, :], out.at[rows, :], sems.at[len(takes) + n])
        )
    for take in takes:
        take.start()
    mark[...] = jnp.zeros_like(mark)
    for n, give in enumerate(gives):
        for take in takes[n : n + 1] if n < 2 else takes[2:]:
            take.wait()
        give.start()
    for give in gives:
        give.wait()


def pack(gate, up, down, after):
    half = gate.shape[0] // 2
    return pl.pallas_call(
        pack_kernel,
        in_specs=[HBM] * 3 + [pl.BlockSpec(memory_space=pl.ANY)],
        out_specs=[HBM, VMEM],
        out_shape=[jax.ShapeDtypeStruct((3 * half, 256), BF16), pltpu.VMEM((8, 128), F32)],
        scratch_shapes=[
            pltpu.VMEM((3 * half, 256), BF16),
            pltpu.SemaphoreType.DMA((5 + half // 256,)),
        ],
        compiler_params=pltpu.CompilerParams(vmem_limit_bytes=56 * MIB),
        cost_estimate=pl.CostEstimate(flops=0, bytes_accessed=12 * MIB, transcendentals=0),
        name="pack",
    )(gate, up, down, after)


def call(kernel, args, outs, name, flops, scratch=()):
    return pl.pallas_call(
        kernel,
        in_specs=[VMEM] * len(args),
        out_specs=[VMEM] * len(outs),
        out_shape=[jax.ShapeDtypeStruct(*out) for out in outs],
        scratch_shapes=list(scratch),
        compiler_params=pltpu.CompilerParams(vmem_limit_bytes=24 * MIB),
        cost_estimate=pl.CostEstimate(flops=flops, bytes_accessed=1 << 20, transcendentals=0),
        name=name,
    )(*args)


def turn_kernel(got, mark, o0, o1, o2, o3):
    rows = got[...].reshape(256, got.shape[2])
    i = iota((256, 1), 0)
    index = (i & 15) * 16 + (i >> 6) * 4 + ((i >> 4) & 3)
    rows = jnp.dot(pick(index, 256), rows, preferred_element_type=F32).astype(BF16)
    for d, out in enumerate((o0, o1, o2, o3)):
        out[...] = rows[d * 64 : d * 64 + 64]


def values_kernel(p0, p1, p2, p3, uv_own, uv_other, out):
    for head, uv in enumerate((uv_own, uv_other)):
        rows = jnp.concatenate(
            [p[head * 32 : head * 32 + 32, :] for p in (p0, p1, p2, p3)], axis=0
        )
        val = jnp.dot(rows, uv[...], preferred_element_type=F32)
        out[:, head * VHEAD : head * VHEAD + VHEAD] = val.astype(BF16)


PARTS = ((0, 64), (64, 96), (96, 128), (128, 160), (160, 192), (192, 224), (224, 256))


LATE = PARTS[:3] + PARTS[5:] + PARTS[3:5]


def put_parts(full, outs, columns, parts):
    for ref, (lo, hi) in zip(outs, parts):
        ref[:, columns] = full[lo:hi].astype(BF16)


def project_kernel(mine, theirs, w, *refs):
    outs, val = refs[:-1], refs[-1]
    _, _, me_t, me_p = coordinates()
    i = iota((128, 1), 0)
    t, b = ((i >> 5) + me_t) & 3, i & 3
    index = ((b - me_p) & 3) * 32 + (i & 0x1C) + t
    sib = jnp.dot(pick(index, 128), theirs[...], preferred_element_type=F32).astype(BF16)
    for d in range(4):
        for s, rows in enumerate((mine[...], sib)):
            at = d * 64 + s * 32
            rows = rows[d * 32 : d * 32 + 32]
            val[at : at + 32, s * VHEAD : s * VHEAD + VHEAD] = rows[:, :VHEAD]
            val[at : at + 32, (1 - s) * VHEAD : (2 - s) * VHEAD] = rows[:, VHEAD:]
    quarter = w.shape[1] // 4
    for q in range(4):
        columns = slice(q * quarter, (q + 1) * quarter)
        full = jnp.dot(val[...], w[:, columns], preferred_element_type=F32)
        put_parts(full, outs, columns, PARTS)


def product_outs(half):
    return [((hi - lo, half), BF16) for lo, hi in PARTS]


def gate_up_kernel(*refs):
    *refs, back, w, packed, part, sent, squares, weight = refs
    count = part.shape[0]
    first = sent.shape[0] - count
    pieces = refs
    if first:
        before, *pieces = refs
        sent[:first, :] = before[...]
    sent = sent.at[pl.ds(first, count), :]
    expert = coordinates()[1]
    half = w.shape[0]
    quarter = half // 4
    sq = jnp.zeros((count, 1), F32)
    for q in range(4):
        columns = slice(q * quarter, (q + 1) * quarter)
        a = jnp.concatenate([p[:, columns] for p in pieces], axis=0)
        up = slice(half + q * quarter, half + (q + 1) * quarter)
        for at, block in ((0, w[columns, :]), (512, packed[columns, :]), (768, packed[up, :])):
            share = jnp.dot(a, block, preferred_element_type=F32)
            spot = slice(at, at + block.shape[1])
            if q == 0:
                part[:, spot] = share
            else:
                part[:, spot] += share
        plain = a.astype(F32) * back[:, columns]
        sq += jnp.sum(plain * plain, axis=1, keepdims=True)
    squares[...] = sq
    sent[:, :1024] = part[...].astype(BF16)
    hi = sq.astype(BF16).astype(F32)
    mid = (sq - hi).astype(BF16).astype(F32)
    lo = sq - hi - mid
    lane = iota((count, 128), 1)
    sent[:, 1024:] = jnp.where(
        lane == 0, hi, jnp.where(lane == 1, mid, jnp.where(lane == 2, lo, 0.0))
    ).astype(BF16)
    n = jnp.concatenate([p[:, half:] for p in pieces], axis=0).astype(F32)
    high = pltpu.roll(n, 128 - TOP, 1)
    low = pltpu.roll(n, 128 - 2 * TOP, 1)
    hit = (lane < TOP) & (n == expert.astype(F32))
    weight[...] = jnp.sum(jnp.where(hit, high + low, 0.0), axis=1, keepdims=True)


def gate_up(before, pieces, back, w, packed):
    count = sum(p.shape[0] for p in pieces)
    rows = count + sum(b.shape[0] for b in before)
    return call(
        gate_up_kernel,
        (*before, *pieces, back, w, packed),
        [((count, 1024), F32), ((rows, 1152), BF16), ((count, 1), F32), ((count, 1), F32)],
        "gate_up",
        count << 23,
    )


def late(d):
    return d ^ (d >> 1)


def down_kernel(p0, q0, w0, p1, q1, w1, got, w, *refs):
    outs, hidden = refs[:-1], refs[-1]
    _, _, me_t, me_p = coordinates()
    i = iota((256, 1), 0)
    d, s, rest = late(i >> 6), (i >> 5) & 1, i & 0x1C
    t, b = (d + me_t) & 3, i & 3
    index = late((b - me_p) & 3) * 64 + (1 - s) * 32 + rest + t
    theirs = jnp.dot(pick(index, 256), got[...], preferred_element_type=F32)
    at = 0
    for part, squares in ((p0, q0), (p1, q1)):
        rows = slice(at, at + part.shape[0])
        at += part.shape[0]
        tail = theirs[rows, 1024:]
        lane = iota(tail.shape, 1)
        sq = squares[...] + jnp.sum(jnp.where(lane < 3, tail, 0.0), axis=1, keepdims=True)
        scale = lax.rsqrt(sq / 7168.0 + 1e-06)
        for block in range(2):
            left, right = block * 512, 512 - block * 512
            gate = (part[:, left : left + 256] + theirs[rows, right : right + 256]) * scale
            left, right = left + 256, right + 256
            up = (part[:, left : left + 256] + theirs[rows, right : right + 256]) * scale
            hidden[rows, block * 256 : block * 256 + 256] = (
                gate / (1.0 + jnp.exp(-gate)) * up
            ).astype(BF16)
    weight = jnp.concatenate([w0[...], w1[...]], axis=0)
    quarter = w.shape[1] // 4
    for q in range(4):
        columns = slice(q * quarter, (q + 1) * quarter)
        full = jnp.dot(hidden[...], w[:, columns], preferred_element_type=F32)
        put_parts(full * weight, outs, columns, LATE)


def add(a, b):
    return (a.astype(F32) + b.astype(F32)).astype(BF16)


def reduce_rows(b0, b1t, b1b, b2t, b2b, b3t, b3b):
    far_left, far_right = ahead(b2t, 1), ahead(b2b, -1)
    left_b, right_t = ahead(b1b, 1), ahead(b3t, -1)
    left_t, right_b = ahead(add(b1t, far_left), 1), ahead(add(b3b, far_right), -1)
    left = jnp.concatenate([left_t, left_b])
    right = jnp.concatenate([right_t, right_b])
    mine = (b0.astype(F32) + left.astype(F32) + right.astype(F32)).astype(BF16)
    mine = mine.reshape(4, 16, mine.shape[1]).swapaxes(0, 1)
    return jnp.sum(plane(mine).astype(F32), axis=0)


def gather_rows(a):
    a0 = plane(jnp.broadcast_to(a, (16, *a.shape)))
    a0 = a0.swapaxes(0, 1).reshape(64, a.shape[1])
    top, bottom = a0[:32], a0[32:]
    left_t, right_b = ahead(top, 1), ahead(bottom, -1)
    left_b, right_t = ahead(bottom, 1), ahead(top, -1)
    return (a0, right_t, right_b, left_t, left_b), (ahead(left_t, 1), ahead(right_b, -1))


def shards(queries, cache, lengths, w_uv, w_out, residual, gain, ids, gates, w_gate, w_up, w_down):
    me = lax.axis_index(AXES)
    core = (me ^ (me >> 1) ^ (me >> 3)) & 1
    half = residual.shape[1] // 2

    def own(w, axis):
        return lax.dynamic_slice_in_dim(w, core * half, half, axis)

    def away(w, axis):
        return lax.dynamic_slice_in_dim(w, (1 - core) * half, half, axis)

    sent, out_other = attend(lengths, queries.swapaxes(1, 2), cache.swapaxes(1, 2), w_out)
    uv_other = swap(w_uv[0])
    packed, mark = pack(w_gate[0], w_up[0], w_down[0], out_other)
    blocks = pl.pallas_call(
        turn_kernel,
        in_specs=[VMEM, VMEM],
        out_specs=[VMEM] * 4,
        out_shape=[jax.ShapeDtypeStruct((64, LATENT), BF16)] * 4,
        compiler_params=pltpu.CompilerParams(vmem_limit_bytes=16 * MIB),
        name="turn",
    )(plane(sent), mark)
    blocks = exchange(blocks)
    out_other = swap(out_other)
    every = slice(None)
    w_out = load(
        (w_out, out_other),
        ((0, 1, slice(0, VHEAD), every), (1, every, slice(VHEAD, 2 * VHEAD), every)),
        (2 * VHEAD, half),
        "load_out",
        8,
    )
    (mine,) = call(
        values_kernel,
        (*blocks, w_uv[0], uv_other),
        [((128, 2 * VHEAD), BF16)],
        "values",
        1 << 25,
    )
    packed = swap(packed)

    gates_hi = gates.astype(BF16)
    gates_lo = (gates - gates_hi.astype(F32)).astype(BF16)
    names = jnp.concatenate(
        [ids.astype(BF16), gates_hi, gates_lo, jnp.zeros((2, 128 - 3 * TOP), BF16)], axis=1
    )
    rows = jnp.concatenate(
        [
            jnp.concatenate([own(residual, 1), names], axis=1),
            swap(jnp.concatenate([away(residual, 1), names], axis=1)),
        ]
    )
    res, names = rows[:, :half].astype(F32), rows[:, half:]

    pieces = call(
        project_kernel,
        (mine, swap(mine), w_out),
        product_outs(half),
        "project",
        1 << 29,
        [pltpu.VMEM((256, 2 * VHEAD), BF16)],
    )
    mixed = res + reduce_rows(*pieces)

    scaled = (mixed * own(gain, 0)).astype(BF16)
    w_gu = load(
        (w_gate[0], w_up[0]),
        (
            (0, 0, every, slice(0, 256)),
            (1, 0, every, slice(256, 512)),
        ),
        (half, 512),
        "load_gate_up",
        42,
    )
    near, far = gather_rows(jnp.concatenate([scaled, names], axis=1))
    back = (1.0 / own(gain, 0)).reshape(1, half)
    p0, sent, q0, w0 = gate_up((), near, back, w_gu, packed)
    p1, sent, q1, w1 = gate_up((sent,), far, back, w_gu, packed)
    w_down = load(
        (w_down[0], packed),
        (
            (0, 1, slice(0, 256), every),
            *(
                (1, slice(2 * half + n, 2 * half + n + 256), slice(256, 512), slice(n, n + 256))
                for n in range(0, half, 256)
            ),
        ),
        (512, half),
        "load_down",
        46,
    )
    pieces = call(
        down_kernel,
        (p0, q0, w0, p1, q1, w1, swap(sent), w_down),
        product_outs(half),
        "down",
        1 << 30,
        [pltpu.VMEM((256, 512), BF16)],
    )
    result = (mixed + reduce_rows(*pieces)).astype(BF16)

    mine, other = result[:2], swap(result[2:])
    return jnp.where(
        core == 0, jnp.concatenate([mine, other], 1), jnp.concatenate([other, mine], 1)
    )


def solution(mesh):
    in_specs = (
        P(("grp", "dev"), None, None),
        P(("grp", "dev"), None, None),
        P(("grp", "dev")),
        P(("grp", "dev"), None, None),
        P(("grp", "dev"), None),
        P(("grp", "dev"), None),
        P(),
        P(("grp", "dev"), None),
        P(("grp", "dev"), None),
        P(("grp", "dev"), None, None),
        P(("grp", "dev"), None, None),
        P(("grp", "dev"), None, None),
    )
    out_specs = P(("grp", "dev"), None)
    return jax.shard_map(shards, mesh=mesh, in_specs=in_specs, out_specs=out_specs, check_vma=False)
```
